256 devices in a mesh: ctx: 32 (over x, z), tp: 8 (over y, core).
Axes of the slice: x: 4, y: 4, z: 8, core: 2. Of those that a mesh axis runs over, the one named last changes fastest.
Arguments:
- queries: bfloat16 [16384, 4096], P('ctx', 'tp'), may hold values from -6 to 6
- prefix_kv: bfloat16 [2, 65536, 1024], P(None, 'ctx', 'tp'), may hold values from -6 to 6
- fresh_kv: bfloat16 [2, 16384, 1024], P(None, 'ctx', 'tp'), may hold values from -6 to 6
- group_blocks: int32 [8, 16], replicated, may hold values from 0 to 639, as said below
- head_pick: int32 [32, 16], replicated, may hold values 0 or 1
- band_start: int32 [32, 4], replicated, may hold values from 0 to 1280, as said below
- band_width: int32 [32, 4], replicated, may hold values from 1 to 256
- o_weight: bfloat16 [4096, 4096], P('tp'), may hold values from -0.125 to 0.125
Outputs:
- projected: bfloat16 [16384, 4096], P('ctx', 'tp')
The draws below stay inside these ranges and needn't reach their ends.
Inputs may be any that keep to these rules, and one draw needn't show every extreme that they name: `group_blocks`: within a row the 16 blocks are distinct; column 0 is block 0 in every row. `band_start`: column 0 is 0 in every row.
All inputs are finite; a program needn't handle non-finite values.
Results may differ from the reference program's by a relative error of at most 0.017.
Values may be sent and summed in bfloat16 or wider, within the bound.
A program may use at most 64 MiB of HBM per device.

```python
import math
import jax
import jax.numpy as jnp
from jax import lax

D = 4096
QH = 32
KVH = 8
HD = 128
BLK = 128
NG = 16
NS = 4
TOK_DEV = 512
BAND_MAX = 256
TOKENS = 16384
PREFIX = 65536
NBLK = 640
N_CTX = 32
N_TP = 8


def shared_signs(key):
    flips = jax.random.bernoulli(key, 0.5, (4, KVH, HD))
    return jnp.where(flips, 1.0, -1.0).astype(jnp.float32)


def draw_queries(key, part):
    signs = shared_signs(key)
    key = jax.random.fold_in(key, 21)
    field = jnp.clip(jax.random.normal(key, (TOKENS, QH * HD), jnp.float32), -6.0, 6.0)
    head_index = jnp.arange(QH, dtype=jnp.int32)
    strength = jnp.array([2.5, 3.5, 4.25], jnp.float32)[head_index % 3]
    head_signs = signs[:, head_index // (QH // KVH), :]
    planted = (strength[None, :, None] * head_signs).reshape(4, QH * HD)
    target_rows = TOKENS - 1 - 2 * jnp.arange(4, dtype=jnp.int32)
    field = field.at[target_rows].set(planted)
    return field.astype(jnp.bfloat16)


def draw_fresh_kv(key, part):
    signs = shared_signs(key)
    key = jax.random.fold_in(key, 22)
    field = jnp.clip(jax.random.normal(key, (2, TOKENS, KVH * HD), jnp.float32), -6.0, 6.0)
    nearer = (5.5 * signs).reshape(4, KVH * HD)
    farther = (5.4375 * signs).reshape(4, KVH * HD)
    target_rows = TOKENS - 1 - 2 * jnp.arange(4, dtype=jnp.int32)
    field = field.at[0, target_rows].set(nearer)
    field = field.at[0, target_rows - 1].set(farther)
    return field.astype(jnp.bfloat16)


def draw_group_blocks(key, part):
    key = jax.random.fold_in(key, 11)
    row_keys = jax.random.split(key, KVH)

    def draw_row(row_key):
        return (jax.random.permutation(row_key, NBLK - 2)[:NG] + 1).astype(jnp.int32)
    block_ids = jax.vmap(draw_row)(row_keys)
    block_ids = block_ids.at[:, 0].set(0)
    return block_ids.at[0, 1].set(NBLK - 1)


def draw_band_start(key, part):
    key = jax.random.fold_in(key, 12)
    starts = jax.random.randint(key, (QH, NS), 1, 3 * TOK_DEV - BAND_MAX + 1, dtype=jnp.int32)
    starts = starts.at[:, 0].set(0)
    return starts.at[0, NS - 1].set(3 * TOK_DEV - BAND_MAX)


def draw_band_width(key, part):
    key = jax.random.fold_in(key, 13)
    widths = jax.random.randint(key, (QH, NS), 1, BAND_MAX + 1, dtype=jnp.int32)
    widths = widths.at[0, 0].set(BAND_MAX)
    return widths.at[1, 0].set(1)


def set_ends(entries, stream_key, smallest, largest):
    longest = entries.shape.index(max(entries.shape))
    spots = []
    for shift in (0, 1):
        where = [jax.random.randint(jax.random.fold_in(stream_key, axis), (), 0, length) for axis, length in enumerate(entries.shape)]
        where[longest] = (where[longest] + shift) % entries.shape[longest]
        spots.append(tuple(where))
    return entries.at[spots[0]].set(smallest).at[spots[1]].set(largest)


def with_spikes(result, key, source, target, blocks, factor):
    def block_of(position):
        return (jnp.arange(result.shape[position]) // (result.shape[position] // blocks)).reshape((-1,) + (1,) * (result.ndim - 1 - position))

    first = jax.random.permutation(key, blocks)[block_of(target)]
    other_side = (block_of(target) + blocks // 2) % blocks
    return jnp.where((block_of(source) == first) | (block_of(source) == other_side), factor * result, result)


def steps_of(rng, extent, cuts, smallest, high):
    def one(axis_at, shards_of):
        draws = jax.random.uniform(jax.random.fold_in(jax.random.fold_in(rng, 6), axis_at), (shards_of,), jnp.float32, smallest / len(cuts), high / len(cuts))
        return jnp.repeat(jnp.exp(draws), extent[axis_at] // shards_of).reshape((-1,) + (1,) * (len(extent) - axis_at - 1))

    factor_of = one(*cuts[0])
    for cut in cuts[1:]:
        factor_of = factor_of * one(*cut)
    return factor_of


def noise(own_key, dims, deviation, most, cuts=(), kind=jnp.bfloat16):
    values = deviation * jax.random.normal(own_key, dims, jnp.float32)
    if cuts:
        values = values * steps_of(own_key, dims, cuts, -0.22, 0.18)
    return jnp.clip(values, -most, most).astype(kind)


def heavy_noise(rng, extent, spread, limit, shards, heavy, kind=jnp.bfloat16):
    result = spread * jax.random.normal(rng, extent, jnp.float32)
    if shards:
        result = result * steps_of(rng, extent, shards, -0.22, 0.18)
    return jnp.clip(with_spikes(result, jax.random.fold_in(rng, 3), *heavy), -limit, limit).astype(kind)


def setup_inputs(seed: int = 0) -> dict:
    keys = jax.random.split(jax.random.key(seed), 9)
    queries = draw_queries(jax.random.fold_in(keys[8], 71), 0)
    prefix_kv = noise(keys[1], (2, PREFIX, KVH * HD), 1.0, 6.0, ((1, 32), (2, 8)))
    fresh_kv = draw_fresh_kv(jax.random.fold_in(keys[8], 71), 0)
    group_blocks = draw_group_blocks(jax.random.fold_in(keys[8], 71), 0)
    head_pick = set_ends((jax.random.randint(keys[4], (QH, NG), 0, 2) < 1).astype(jnp.int32), jax.random.fold_in(keys[4], 1), 0, 1)
    band_start = draw_band_start(jax.random.fold_in(keys[8], 71), 0)
    band_width = draw_band_width(jax.random.fold_in(keys[8], 71), 0)
    o_weight = heavy_noise(keys[7], (QH * HD, D), (QH * HD) ** -0.5, 0.125, ((0, 8),), (0, 1, 8, 2.0))
    return dict(queries=queries, prefix_kv=prefix_kv, fresh_kv=fresh_kv, group_blocks=group_blocks, head_pick=head_pick, band_start=band_start, band_width=band_width, o_weight=o_weight)


def reference(queries, prefix_kv, fresh_kv, group_blocks, head_pick, band_start, band_width, o_weight):
    length = PREFIX + TOKENS
    per_group = QH // KVH
    score_scale = 1.0 / math.sqrt(HD)
    all_kv = jnp.concatenate([prefix_kv, fresh_kv], axis=1).reshape(2, length, KVH, HD)
    head_group = jnp.arange(QH, dtype=jnp.int32) // per_group
    slot_pos = (group_blocks[:, :, None] * BLK + jnp.arange(BLK, dtype=jnp.int32)[None, None, :]).reshape(KVH, NG * BLK)
    vert_kv = jnp.stack([all_kv[:, slot_pos[group_index], group_index, :] for group_index in range(KVH)], axis=1)
    head_vert = vert_kv[:, head_group].astype(jnp.float32)
    head_slots = slot_pos[head_group]
    pick_flag = head_pick == 1
    slot_pick = jnp.repeat(pick_flag, BLK, axis=1)
    head_blocks = group_blocks[head_group]
    query_all = queries.reshape(TOKENS, QH, HD)

    def one_shard(shard_index):
        query_block = lax.dynamic_slice_in_dim(query_all, shard_index * TOK_DEV, TOK_DEV, 0).astype(jnp.float32)
        query_pos = PREFIX + shard_index * TOK_DEV + jnp.arange(TOK_DEV, dtype=jnp.int32)
        window_first = PREFIX + (shard_index - 3) * TOK_DEV
        window = lax.dynamic_slice_in_dim(all_kv, window_first, 4 * TOK_DEV, 1)[:, :, head_group].astype(jnp.float32)
        window_pos = window_first + jnp.arange(4 * TOK_DEV, dtype=jnp.int32)
        vert_mask = slot_pick[:, None, :] & (head_slots[:, None, :] <= query_pos[None, :, None])
        window_block = window_pos // BLK
        in_vert = jnp.any((window_block[None, :, None] == head_blocks[:, None, :]) & pick_flag[:, None, :], axis=2)
        distance = query_pos[:, None] - window_pos[None, :]
        in_band = jnp.zeros((QH, TOK_DEV, 4 * TOK_DEV), jnp.bool_)
        for band_index in range(NS):
            band_lower = band_start[:, band_index][:, None, None]
            band_upper = band_lower + band_width[:, band_index][:, None, None]
            in_band = in_band | (distance[None] >= band_lower) & (distance[None] < band_upper)
        fresh_key = (window_pos >= PREFIX)[None, None, :]
        band_mask = in_band & jnp.logical_not(in_vert)[:, None, :] & (distance >= 0)[None] & fresh_key
        vert_scores = jnp.einsum('thd,hkd->htk', query_block, head_vert[0]) * score_scale
        band_scores = jnp.einsum('thd,khd->htk', query_block, window[0]) * score_scale
        row_max = jnp.maximum(lax.optimization_barrier(jnp.max(jnp.where(vert_mask, vert_scores, -jnp.inf), axis=2, keepdims=True)), lax.optimization_barrier(jnp.max(jnp.where(band_mask, band_scores, -jnp.inf), axis=2, keepdims=True)))
        vert_exp = jnp.where(vert_mask, jnp.exp(vert_scores - row_max), 0.0)
        band_exp = jnp.where(band_mask, jnp.exp(band_scores - row_max), 0.0)
        row_total = lax.optimization_barrier(jnp.sum(vert_exp, axis=2, keepdims=True)) + lax.optimization_barrier(jnp.sum(band_exp, axis=2, keepdims=True))
        vert_probs = lax.optimization_barrier((vert_exp / row_total).astype(jnp.bfloat16)).astype(jnp.float32)
        band_probs = lax.optimization_barrier((band_exp / row_total).astype(jnp.bfloat16)).astype(jnp.float32)
        head_out = jnp.einsum('htk,hkd->thd', vert_probs, head_vert[1]) + jnp.einsum('htk,khd->thd', band_probs, window[1])
        return head_out.astype(jnp.bfloat16).reshape(TOK_DEV, QH * HD)
    attended = lax.map(one_shard, jnp.arange(N_CTX, dtype=jnp.int32)).reshape(TOKENS, QH * HD)
    heads_per = QH * HD // N_TP
    summed = jnp.zeros((TOKENS, D), jnp.float32)
    for tp_group in range(N_TP):
        columns = attended[:, tp_group * heads_per:(tp_group + 1) * heads_per]
        weights = o_weight[tp_group * heads_per:(tp_group + 1) * heads_per]
        group_term = jnp.dot(columns, weights, preferred_element_type=jnp.float32).astype(jnp.bfloat16)
        summed = summed + lax.optimization_barrier(group_term).astype(jnp.float32)
    return summed.astype(jnp.bfloat16)
```

```python
import functools
import math

import jax
import jax.numpy as jnp
from jax import lax
from jax.experimental import pallas as pl
from jax.experimental.pallas import tpu as pltpu
from jax.sharding import PartitionSpec as P

QH = 32
KVH = 8
HD = 128
BLK = 128
NG = 16
NS = 4
TOK = 512
PREFIX_BLOCKS = 512
WINDOW_TILES = 13
TILES = NG + WINDOW_TILES
CHUNKS = TOK // BLK
HEADS = QH // KVH
OFF = -1e30
EXP_SCALE = math.log2(math.e) / math.sqrt(HD)
OPEN, SHUT, CAUSAL, FIRST_BAND = 0, 1, 2, 3
BIAS_TILES = FIRST_BAND + HEADS * WINDOW_TILES


def pick_kernel(prefix_blocks, fresh_blocks, blocks_ref, prefix_ref, fresh_ref, out_ref):
    ctx = lax.axis_index("ctx")
    group = lax.axis_index("tp")
    for slot in range(NG):
        block = blocks_ref[group, slot]
        at_prefix = block - ctx * prefix_blocks
        at_fresh = block - PREFIX_BLOCKS - ctx * fresh_blocks
        in_prefix = (at_prefix >= 0) & (at_prefix < prefix_blocks) & (block < PREFIX_BLOCKS)
        in_fresh = (at_fresh >= 0) & (at_fresh < fresh_blocks)
        row_prefix = pl.multiple_of(jnp.clip(at_prefix, 0, prefix_blocks - 1) * BLK, BLK)
        row_fresh = pl.multiple_of(jnp.clip(at_fresh, 0, fresh_blocks - 1) * BLK, BLK)
        for part in range(2):
            from_prefix = prefix_ref[part, pl.ds(row_prefix, BLK), :]
            from_fresh = fresh_ref[part, pl.ds(row_fresh, BLK), :]
            zero = jnp.zeros_like(from_prefix)
            value = jnp.where(in_prefix, from_prefix, jnp.where(in_fresh, from_fresh, zero))
            out_ref[part, slot * BLK : (slot + 1) * BLK, :] = value


def make_bias(starts_ref, widths_ref, first_head, bias_ref):
    rows = lax.broadcasted_iota(jnp.int32, (BLK, BLK), 0)
    cols = lax.broadcasted_iota(jnp.int32, (BLK, BLK), 1)
    bias_ref[OPEN] = jnp.zeros((BLK, BLK), jnp.float32)
    bias_ref[SHUT] = jnp.full((BLK, BLK), OFF, jnp.float32)
    bias_ref[CAUSAL] = jnp.where(rows >= cols, 0.0, OFF)

    @pl.loop(0, HEADS)
    def per_head(head):
        @pl.loop(0, WINDOW_TILES)
        def per_tile(tile):
            distance = (rows - cols) + tile * BLK
            inside = jnp.zeros((BLK, BLK), jnp.bool_)
            for band in range(NS):
                start = starts_ref[first_head + head, band]
                width = widths_ref[first_head + head, band]
                inside = inside | ((distance >= start) & (distance < start + width))
            bias_ref[FIRST_BAND + head * WINDOW_TILES + tile] = jnp.where(inside, 0.0, OFF)


def attend_kernel(
    idx_ref, starts_ref, widths_ref, q_ref, vert_ref, win_ref, out_ref, bias_ref, s_ref, q_s, m_s, l_s, acc_s
):
    make_bias(starts_ref, widths_ref, lax.axis_index("tp") * HEADS, bias_ref)
    contract = (((1,), (1,)), ((), ()))

    @pl.loop(0, CHUNKS)
    def per_chunk(chunk):
        row0 = pl.multiple_of(chunk * BLK, BLK)
        for head in range(HEADS):
            q_s[head * BLK : (head + 1) * BLK, :] = q_ref[pl.ds(row0, BLK), head * HD : (head + 1) * HD]
        m_s[...] = jnp.full_like(m_s, OFF)

        def score(keys, tile, column, count):
            s = lax.dot_general(q_s[...], keys, contract, preferred_element_type=jnp.float32)
            for head in range(HEADS):
                rows = slice(head * BLK, (head + 1) * BLK)
                best = m_s[rows, :]
                for part in range(count):
                    piece = s[rows, part * BLK : (part + 1) * BLK]
                    piece = piece + bias_ref[idx_ref[chunk, head, tile + part]]
                    s_ref[rows, pl.ds(pl.multiple_of(column + part * BLK, BLK), BLK)] = piece
                    best = jnp.maximum(best, piece)
                m_s[rows, :] = best

        @pl.loop(0, NG // 2)
        def vertical(step):
            at = pl.multiple_of(step * 2 * BLK, 2 * BLK)
            score(vert_ref[0, pl.ds(at, 2 * BLK), :], step * 2, at, 2)

        @pl.loop(0, WINDOW_TILES // 2)
        def window(step):
            at = pl.multiple_of(step * 2 * BLK, 2 * BLK)
            score(win_ref[0, pl.ds(row0 + at, 2 * BLK), :], NG + step * 2, NG * BLK + at, 2)

        last = (WINDOW_TILES - 1) * BLK
        score(win_ref[0, pl.ds(row0 + last, BLK), :], TILES - 1, NG * BLK + last, 1)

        m_s[...] = jnp.broadcast_to(jnp.max(m_s[...], axis=1, keepdims=True), m_s.shape)
        l_s[...] = jnp.zeros_like(l_s)
        acc_s[...] = jnp.zeros_like(acc_s)

        def weigh(values, column, count):
            top = m_s[...]
            total = l_s[...]
            probs = []
            for part in range(count):
                piece = s_ref[:, pl.ds(pl.multiple_of(column + part * BLK, BLK), BLK)]
                piece = jnp.exp2((piece - top) * EXP_SCALE)
                total = total + piece
                probs.append(piece.astype(jnp.bfloat16))
            l_s[...] = total
            p = probs[0] if count == 1 else jnp.concatenate(probs, axis=1)
            acc_s[...] += jnp.dot(p, values, preferred_element_type=jnp.float32)

        @pl.loop(0, NG // 2)
        def vertical_values(step):
            at = pl.multiple_of(step * 2 * BLK, 2 * BLK)
            weigh(vert_ref[1, pl.ds(at, 2 * BLK), :], at, 2)

        @pl.loop(0, WINDOW_TILES // 2)
        def window_values(step):
            at = pl.multiple_of(step * 2 * BLK, 2 * BLK)
            weigh(win_ref[1, pl.ds(row0 + at, 2 * BLK), :], NG * BLK + at, 2)

        weigh(win_ref[1, pl.ds(row0 + last, BLK), :], NG * BLK + last, 1)
        result = acc_s[...] / jnp.sum(l_s[...], axis=1, keepdims=True)
        for head in range(HEADS):
            out_ref[pl.ds(row0, BLK), head * HD : (head + 1) * HD] = result[
                head * BLK : (head + 1) * BLK, :
            ].astype(jnp.bfloat16)


def bias_index(group_blocks, head_pick, ctx, tp):
    blocks = lax.dynamic_index_in_dim(group_blocks, tp, 0, keepdims=False)
    picks = lax.dynamic_slice_in_dim(head_pick, tp * HEADS, HEADS, 0) == 1
    chunk = jnp.arange(CHUNKS, dtype=jnp.int32)[:, None, None]
    own = PREFIX_BLOCKS + ctx * CHUNKS + chunk
    listed = blocks[None, None, :]
    vertical = jnp.where(listed < own, OPEN, jnp.where(listed == own, CAUSAL, SHUT))
    vertical = jnp.where(picks[None], vertical, SHUT)
    tile = jnp.arange(WINDOW_TILES, dtype=jnp.int32)[None, None, :]
    block = own + tile - (WINDOW_TILES - 1)
    seen = jnp.any((block[..., None] == blocks) & picks[None, :, None, :], axis=-1)
    head = jnp.arange(HEADS, dtype=jnp.int32)[None, :, None]
    band = FIRST_BAND + head * WINDOW_TILES + (WINDOW_TILES - 1 - tile)
    window = jnp.where(seen | (block < PREFIX_BLOCKS), SHUT, band)
    return jnp.concatenate([vertical, window], axis=-1).astype(jnp.int32)


def passed_along(block, axis, distance):
    devices = range(lax.axis_size(axis))
    route = [(i - distance, i) for i in devices if i - distance in devices]
    return lax.ppermute(block, axis, route)


VMEM = pl.BlockSpec(memory_space=pltpu.VMEM)
SMEM = pl.BlockSpec(memory_space=pltpu.SMEM)


def local(queries, prefix_kv, fresh_kv, group_blocks, head_pick, band_start, band_width, o_weight):
    ctx = lax.axis_index("ctx")
    tp = lax.axis_index("tp")
    picked = pl.pallas_call(
        functools.partial(pick_kernel, prefix_kv.shape[1] // BLK, fresh_kv.shape[1] // BLK),
        out_shape=jax.ShapeDtypeStruct((2, NG * BLK, HD), jnp.bfloat16),
        in_specs=[SMEM, VMEM, VMEM],
        out_specs=VMEM,
        compiler_params=pltpu.CompilerParams(vmem_limit_bytes=16 * 2**20),
    )(group_blocks, prefix_kv, fresh_kv)
    vert = lax.psum(picked, "ctx")
    earlier = [passed_along(fresh_kv, "ctx", back) for back in (3, 2, 1)]
    window = jnp.concatenate(earlier + [fresh_kv], axis=1)
    index = bias_index(group_blocks, head_pick, ctx, tp)
    rows = HEADS * BLK
    attended = pl.pallas_call(
        attend_kernel,
        out_shape=jax.ShapeDtypeStruct((TOK, HEADS * HD), jnp.bfloat16),
        in_specs=[SMEM, SMEM, SMEM, VMEM, VMEM, VMEM],
        out_specs=VMEM,
        scratch_shapes=[
            pltpu.VMEM((BIAS_TILES, BLK, BLK), jnp.float32),
            pltpu.VMEM((rows, TILES * BLK), jnp.float32),
            pltpu.VMEM((rows, HD), jnp.bfloat16),
            pltpu.VMEM((rows, BLK), jnp.float32),
            pltpu.VMEM((rows, BLK), jnp.float32),
            pltpu.VMEM((rows, HD), jnp.float32),
        ],
        compiler_params=pltpu.CompilerParams(vmem_limit_bytes=32 * 2**20),
    )(index, band_start, band_width, queries, vert, window)
    projected = jnp.dot(attended, o_weight, preferred_element_type=jnp.float32)
    return lax.psum_scatter(projected.astype(jnp.bfloat16), "tp", scatter_dimension=1, tiled=True)


def solution(mesh):
    return jax.shard_map(
        local,
        mesh=mesh,
        in_specs=(
            P("ctx", "tp"),
            P(None, "ctx", "tp"),
            P(None, "ctx", "tp"),
            P(),
            P(),
            P(),
            P(),
            P("tp", None),
        ),
        out_specs=P("ctx", "tp"),
        check_vma=False,
    )
```

```python
import functools
import math

import jax
import jax.numpy as jnp
from jax import lax
from jax.experimental import pallas as pl
from jax.experimental.pallas import tpu as pltpu
from jax.sharding import PartitionSpec as P

QH = 32
KVH = 8
HD = 128
BLK = 128
NG = 16
NS = 4
TOK = 512
PREFIX_BLOCKS = 512
WINDOW_TILES = 13
TILES = NG + WINDOW_TILES
CHUNKS = TOK // BLK
HEADS = QH // KVH
X_SIZE = 4
Z_SIZE = 8
QUARTER = NG * BLK // X_SIZE
HALF = QUARTER // 2
PIECE = QUARTER // Z_SIZE
PREFIX_DEV = 16
FRESH_DEV = 4
MESH = pl.DeviceIdType.MESH
OFF = -1e30
EXP_SCALE = math.log2(math.e) / math.sqrt(HD)
OPEN, SHUT, CAUSAL, FIRST_BAND = 0, 1, 2, 3
BIAS_TILES = FIRST_BAND + HEADS * WINDOW_TILES


def make_bias(starts_ref, widths_ref, first_head, bias_ref):
    rows = lax.broadcasted_iota(jnp.int32, (BLK, BLK), 0)
    cols = lax.broadcasted_iota(jnp.int32, (BLK, BLK), 1)
    bias_ref[OPEN] = jnp.zeros((BLK, BLK), jnp.float32)
    bias_ref[SHUT] = jnp.full((BLK, BLK), OFF, jnp.float32)
    bias_ref[CAUSAL] = jnp.where(rows >= cols, 0.0, OFF)

    @pl.loop(0, HEADS)
    def per_head(head):
        @pl.loop(0, WINDOW_TILES)
        def per_tile(tile):
            distance = (rows - cols) + tile * BLK
            inside = jnp.zeros((BLK, BLK), jnp.bool_)
            for band in range(NS):
                start = starts_ref[first_head + head, band]
                width = widths_ref[first_head + head, band]
                inside = inside | ((distance >= start) & (distance < start + width))
            bias_ref[FIRST_BAND + head * WINDOW_TILES + tile] = jnp.where(inside, 0.0, OFF)


def attend(idx_ref, q_ref, vert_ref, win_ref, out_ref, bias_ref, s_ref, q_s, m_s, l_s, acc_s):
    contract = (((1,), (1,)), ((), ()))

    @pl.loop(0, CHUNKS)
    def per_chunk(chunk):
        row0 = pl.multiple_of(chunk * BLK, BLK)
        for head in range(HEADS):
            q_s[head * BLK : (head + 1) * BLK, :] = q_ref[pl.ds(row0, BLK), head * HD : (head + 1) * HD]
        m_s[...] = jnp.full_like(m_s, OFF)

        def score(keys, tile, column, count):
            s = lax.dot_general(q_s[...], keys, contract, preferred_element_type=jnp.float32)
            for head in range(HEADS):
                rows = slice(head * BLK, (head + 1) * BLK)
                best = m_s[rows, :]
                for part in range(count):
                    piece = s[rows, part * BLK : (part + 1) * BLK]
                    piece = piece + bias_ref[idx_ref[chunk, head, tile + part]]
                    s_ref[rows, pl.ds(pl.multiple_of(column + part * BLK, BLK), BLK)] = piece
                    best = jnp.maximum(best, piece)
                m_s[rows, :] = best

        @pl.loop(0, NG // 2)
        def vertical(step):
            at = pl.multiple_of(step * 2 * BLK, 2 * BLK)
            score(vert_ref[0, pl.ds(at, 2 * BLK), :], step * 2, at, 2)

        @pl.loop(0, WINDOW_TILES // 2)
        def window(step):
            at = pl.multiple_of(step * 2 * BLK, 2 * BLK)
            score(win_ref[0, pl.ds(row0 + at, 2 * BLK), :], NG + step * 2, NG * BLK + at, 2)

        last = (WINDOW_TILES - 1) * BLK
        score(win_ref[0, pl.ds(row0 + last, BLK), :], TILES - 1, NG * BLK + last, 1)

        m_s[...] = jnp.broadcast_to(jnp.max(m_s[...], axis=1, keepdims=True), m_s.shape)
        l_s[...] = jnp.zeros_like(l_s)
        acc_s[...] = jnp.zeros_like(acc_s)

        def weigh(values, column, count):
            top = m_s[...]
            total = l_s[...]
            probs = []
            for part in range(count):
                piece = s_ref[:, pl.ds(pl.multiple_of(column + part * BLK, BLK), BLK)]
                piece = jnp.exp2((piece - top) * EXP_SCALE)
                total = total + piece
                probs.append(piece.astype(jnp.bfloat16))
            l_s[...] = total
            p = probs[0] if count == 1 else jnp.concatenate(probs, axis=1)
            acc_s[...] += jnp.dot(p, values, preferred_element_type=jnp.float32)

        @pl.loop(0, NG // 2)
        def vertical_values(step):
            at = pl.multiple_of(step * 2 * BLK, 2 * BLK)
            weigh(vert_ref[1, pl.ds(at, 2 * BLK), :], at, 2)

        @pl.loop(0, WINDOW_TILES // 2)
        def window_values(step):
            at = pl.multiple_of(step * 2 * BLK, 2 * BLK)
            weigh(win_ref[1, pl.ds(row0 + at, 2 * BLK), :], NG * BLK + at, 2)

        weigh(win_ref[1, pl.ds(row0 + last, BLK), :], NG * BLK + last, 1)
        result = acc_s[...] / jnp.sum(l_s[...], axis=1, keepdims=True)
        for head in range(HEADS):
            out_ref[pl.ds(row0, BLK), head * HD : (head + 1) * HD] = result[
                head * BLK : (head + 1) * BLK, :
            ].astype(jnp.bfloat16)


def bias_index(group_blocks, head_pick, ctx, tp):
    blocks = lax.dynamic_index_in_dim(group_blocks, tp, 0, keepdims=False)
    picks = lax.dynamic_slice_in_dim(head_pick, tp * HEADS, HEADS, 0) == 1
    chunk = jnp.arange(CHUNKS, dtype=jnp.int32)[:, None, None]
    own = PREFIX_BLOCKS + ctx * CHUNKS + chunk
    listed = blocks[None, None, :]
    vertical = jnp.where(listed < own, OPEN, jnp.where(listed == own, CAUSAL, SHUT))
    vertical = jnp.where(picks[None], vertical, SHUT)
    tile = jnp.arange(WINDOW_TILES, dtype=jnp.int32)[None, None, :]
    block = own + tile - (WINDOW_TILES - 1)
    seen = jnp.any((block[..., None] == blocks) & picks[None, :, None, :], axis=-1)
    head = jnp.arange(HEADS, dtype=jnp.int32)[None, :, None]
    band = FIRST_BAND + head * WINDOW_TILES + (WINDOW_TILES - 1 - tile)
    window = jnp.where(seen | (block < PREFIX_BLOCKS), SHUT, band)
    return jnp.concatenate([vertical, window], axis=-1).astype(jnp.int32)


def pick(blocks_ref, prefix_ref, fresh_ref, out_ref, part):
    ctx = lax.axis_index("ctx")
    group = lax.axis_index("tp")
    for slot in range(NG):
        block = blocks_ref[group, slot]
        at_prefix = block - ctx * PREFIX_DEV
        at_fresh = block - PREFIX_BLOCKS - ctx * FRESH_DEV
        in_prefix = (at_prefix >= 0) & (at_prefix < PREFIX_DEV) & (block < PREFIX_BLOCKS)
        in_fresh = (at_fresh >= 0) & (at_fresh < FRESH_DEV)
        from_prefix = prefix_ref[part, jnp.clip(at_prefix, 0, PREFIX_DEV - 1)]
        from_fresh = fresh_ref[part, jnp.clip(at_fresh, 0, FRESH_DEV - 1)]
        zero = jnp.zeros_like(from_prefix)
        value = jnp.where(in_prefix, from_prefix, jnp.where(in_fresh, from_fresh, zero))
        out_ref[part, slot * BLK : (slot + 1) * BLK, :] = value


class Sends:
    def __init__(self, send_sem, recv_sem):
        self.send_sem, self.recv_sem, self.used, self.started = send_sem, recv_sem, 0, []

    def make(self, src, dst, device):
        slot = self.used
        self.used += 1
        return pltpu.make_async_remote_copy(
            src_ref=src,
            dst_ref=dst,
            send_sem=self.send_sem.at[slot],
            recv_sem=self.recv_sem.at[slot],
            device_id=device,
            device_id_type=MESH,
        )

    def start(self, src, dst, device):
        copy = self.make(src, dst, device)
        copy.start()
        self.started.append(copy)
        return copy

    def finish(self):
        for copy in self.started:
            copy.wait_send()


def collect(blocks_ref, prefix_ref, fresh_ref, vert_ref, win_ref, mine, far_in, near_in, piece_in, sends):
    ctx = lax.axis_index("ctx")
    tp = lax.axis_index("tp")
    x, z = ctx // Z_SIZE, ctx % Z_SIZE
    x_far, x_right, x_left = (x + 2) % X_SIZE, (x + 1) % X_SIZE, (x + 3) % X_SIZE
    right = (x_right * Z_SIZE + z, tp)
    left = (x_left * Z_SIZE + z, tp)
    along = [(x * Z_SIZE + (z + k) % Z_SIZE, tp) for k in range(1, Z_SIZE)]
    size = X_SIZE * Z_SIZE
    after = ((ctx + 1) % size, tp)
    before = ((ctx + size - 1) % size, tp)

    barrier = pltpu.get_barrier_semaphore()
    partners = [right, left] + along + [after, before]
    for device in partners:
        pl.semaphore_signal(barrier, inc=1, device_id=device, device_id_type=MESH)
    for part in range(2):
        pick(blocks_ref, prefix_ref, fresh_ref, mine, part)
        for block in range(FRESH_DEV):
            win_ref[part, 3 * TOK + block * BLK : 3 * TOK + (block + 1) * BLK, :] = fresh_ref[part, block]
    pl.semaphore_wait(barrier, len(partners))

    def rows(start, count):
        return pl.ds(pl.multiple_of(start, PIECE), count)

    def hand_on(part, age):
        return sends.start(
            win_ref.at[part, pl.ds((3 - age) * TOK, TOK), :],
            win_ref.at[part, pl.ds((2 - age) * TOK, TOK), :],
            after,
        )

    far, near, window = {}, {}, {}
    for part in range(2):
        far[part] = [
            sends.start(mine.at[part, rows(x_far * QUARTER, HALF), :], far_in.at[part, 0], right),
            sends.start(mine.at[part, rows(x_far * QUARTER + HALF, HALF), :], far_in.at[part, 1], left),
        ]
        near[part] = [
            sends.start(
                mine.at[part, rows(x_right * QUARTER + HALF, HALF), :], near_in.at[part, 0, pl.ds(HALF, HALF), :], right
            ),
            sends.start(mine.at[part, rows(x_left * QUARTER, HALF), :], near_in.at[part, 1, pl.ds(0, HALF), :], left),
        ]
        window[part, 0] = hand_on(part, 0)
    for part in range(2):
        far[part][0].wait_recv()
        mine[part, rows(x_right * QUARTER, HALF), :] += far_in[part, 0]
        near[part].append(
            sends.start(mine.at[part, rows(x_right * QUARTER, HALF), :], near_in.at[part, 0, pl.ds(0, HALF), :], right)
        )
        far[part][1].wait_recv()
        mine[part, rows(x_left * QUARTER + HALF, HALF), :] += far_in[part, 1]
        near[part].append(
            sends.start(
                mine.at[part, rows(x_left * QUARTER + HALF, HALF), :], near_in.at[part, 1, pl.ds(HALF, HALF), :], left
            )
        )
    pieces = {}
    for part in range(2):
        for copy in near[part]:
            copy.wait_recv()
        own = rows(x * QUARTER, QUARTER)
        mine[part, own, :] = mine[part, own, :] + near_in[part, 0] + near_in[part, 1]
        pieces[part] = [
            sends.start(
                mine.at[part, rows(x * QUARTER + (z + k) % Z_SIZE * PIECE, PIECE), :],
                piece_in.at[part, k - 1],
                along[k - 1],
            )
            for k in range(1, Z_SIZE)
        ]
        window[part, 0].wait_recv()
        window[part, 1] = hand_on(part, 1)
    gathered = {}
    for part in range(2):
        at = rows(x * QUARTER + z * PIECE, PIECE)
        total = mine[part, at, :]
        for k in range(1, Z_SIZE):
            pieces[part][k - 1].wait_recv()
            total = total + piece_in[part, k - 1]
        vert_ref[part, at, :] = total
        gathered[part] = [
            sends.start(vert_ref.at[part, at, :], vert_ref.at[part, at, :], along[k - 1]) for k in range(1, Z_SIZE)
        ]
        window[part, 1].wait_recv()
        window[part, 2] = hand_on(part, 2)
    spread = {}
    for part in range(2):
        for copy in gathered[part]:
            copy.wait_recv()
        spread[part] = []
        for start in (0, HALF):
            at = rows(x * QUARTER + start, HALF)
            for device in (right, left):
                spread[part].append(sends.start(vert_ref.at[part, at, :], vert_ref.at[part, at, :], device))
    relayed = []
    for part in range(2):
        top_right, top_left, low_right, low_left = spread[part]
        top_right.wait_recv()
        at = rows(x_left * QUARTER, HALF)
        relayed.append(sends.start(vert_ref.at[part, at, :], vert_ref.at[part, at, :], right))
        low_left.wait_recv()
        at = rows(x_right * QUARTER + HALF, HALF)
        relayed.append(sends.start(vert_ref.at[part, at, :], vert_ref.at[part, at, :], left))
        top_left.wait_recv()
        low_right.wait_recv()
    for copy in relayed:
        copy.wait_recv()
    for part in range(2):
        window[part, 2].wait_recv()
    sends.finish()


def attend_kernel(
    blocks_ref, idx_ref, starts_ref, widths_ref, q_ref, prefix_ref, fresh_ref, out_ref,
    mine, far_in, near_in, piece_in, vert_ref, win_ref, send_sem, recv_sem,
    bias_ref, s_ref, q_s, m_s, l_s, acc_s,
):
    sends = Sends(send_sem, recv_sem)
    collect(blocks_ref, prefix_ref, fresh_ref, vert_ref, win_ref, mine, far_in, near_in, piece_in, sends)
    make_bias(starts_ref, widths_ref, lax.axis_index("tp") * HEADS, bias_ref)
    attend(idx_ref, q_ref, vert_ref, win_ref, out_ref, bias_ref, s_ref, q_s, m_s, l_s, acc_s)


VMEM = pl.BlockSpec(memory_space=pltpu.VMEM)
SMEM = pl.BlockSpec(memory_space=pltpu.SMEM)
COPIES = 64


def project_kernel(att_ref, w_ref, out_ref, w_in, att_in, mine, far_in, near_in, send_sem, recv_sem):
    ctx = lax.axis_index("ctx")
    tp = lax.axis_index("tp")
    y, core = tp // 2, tp % 2
    y_far, y_right, y_left = (y + 2) % 4, (y + 1) % 4, (y + 3) % 4
    pair = (ctx, y * 2 + (1 - core))
    right = (ctx, y_right * 2 + core)
    left = (ctx, y_left * 2 + core)
    barrier = pltpu.get_barrier_semaphore()
    for device in (pair, right, left):
        pl.semaphore_signal(barrier, inc=1, device_id=device, device_id_type=MESH)
    pl.semaphore_wait(barrier, 3)
    sends = Sends(send_sem, recv_sem)
    att = sends.start(att_ref, att_in, pair)
    weights = [
        sends.start(w_ref.at[:, pl.ds(pl.multiple_of((to * 2 + 1 - core) * TOK, TOK), TOK)], w_in.at[to], pair)
        for to in range(4)
    ]
    att.wait_recv()
    for copy in weights:
        copy.wait_recv()

    def term(to, start, count):
        columns = pl.ds(pl.multiple_of((to * 2 + core) * TOK, TOK), TOK)
        at = slice(start, start + count)
        total = jnp.dot(att_ref[at, :], w_ref[:, columns], preferred_element_type=jnp.float32)
        return total + jnp.dot(att_in[at, :], w_in[to], preferred_element_type=jnp.float32)

    half = TOK // 2
    top, low = pl.ds(0, half), pl.ds(half, half)
    mine[0, :half, :] = term(y_far, 0, half).astype(jnp.bfloat16)
    far_top = sends.start(mine.at[0, top, :], far_in.at[0], right)
    mine[0, half:, :] = term(y_far, half, half).astype(jnp.bfloat16)
    far_low = sends.start(mine.at[0, low, :], far_in.at[1], left)
    mine[1, half:, :] = term(y_right, half, half).astype(jnp.bfloat16)
    right_low = sends.start(mine.at[1, low, :], near_in.at[0, low, :], right)
    mine[2, :half, :] = term(y_left, 0, half).astype(jnp.bfloat16)
    left_top = sends.start(mine.at[2, top, :], near_in.at[1, top, :], left)
    near = term(y_right, 0, half)
    far_top.wait_recv()
    mine[1, :half, :] = (near + far_in[0].astype(jnp.float32)).astype(jnp.bfloat16)
    right_top = sends.start(mine.at[1, top, :], near_in.at[0, top, :], right)
    near = term(y_left, half, half)
    far_low.wait_recv()
    mine[2, half:, :] = (near + far_in[1].astype(jnp.float32)).astype(jnp.bfloat16)
    left_low = sends.start(mine.at[2, low, :], near_in.at[1, low, :], left)
    own_top = term(y, 0, half)
    own_low = term(y, half, half)

    def add(own, at):
        from_left = near_in[0, at, :].astype(jnp.float32)
        from_right = near_in[1, at, :].astype(jnp.float32)
        out_ref[at, :] = (own + from_left + from_right).astype(jnp.bfloat16)

    left_top.wait_recv()
    right_top.wait_recv()
    add(own_top, slice(0, half))
    right_low.wait_recv()
    left_low.wait_recv()
    add(own_low, slice(half, TOK))
    sends.finish()


def local(queries, prefix_kv, fresh_kv, group_blocks, head_pick, band_start, band_width, o_weight):
    ctx = lax.axis_index("ctx")
    tp = lax.axis_index("tp")
    index = bias_index(group_blocks, head_pick, ctx, tp)
    rows = HEADS * BLK
    bf16 = jnp.bfloat16
    attended = pl.pallas_call(
        attend_kernel,
        out_shape=jax.ShapeDtypeStruct((TOK, HEADS * HD), bf16),
        in_specs=[SMEM, SMEM, SMEM, SMEM, VMEM, VMEM, VMEM],
        out_specs=VMEM,
        scratch_shapes=[
            pltpu.VMEM((2, NG * BLK, HD), bf16),
            pltpu.VMEM((2, 2, HALF, HD), bf16),
            pltpu.VMEM((2, 2, QUARTER, HD), bf16),
            pltpu.VMEM((2, Z_SIZE - 1, PIECE, HD), bf16),
            pltpu.VMEM((2, NG * BLK, HD), bf16),
            pltpu.VMEM((2, 4 * TOK, HD), bf16),
            pltpu.SemaphoreType.DMA((COPIES,)),
            pltpu.SemaphoreType.DMA((COPIES,)),
            pltpu.VMEM((BIAS_TILES, BLK, BLK), jnp.float32),
            pltpu.VMEM((rows, TILES * BLK), jnp.float32),
            pltpu.VMEM((rows, HD), bf16),
            pltpu.VMEM((rows, BLK), jnp.float32),
            pltpu.VMEM((rows, BLK), jnp.float32),
            pltpu.VMEM((rows, HD), jnp.float32),
        ],
        compiler_params=pltpu.CompilerParams(
            vmem_limit_bytes=48 * 2**20, collective_id=0, has_side_effects=True
        ),
    )(
        group_blocks,
        index,
        band_start,
        band_width,
        queries,
        prefix_kv.reshape(2, PREFIX_DEV, BLK, HD),
        fresh_kv.reshape(2, FRESH_DEV, BLK, HD),
    )
    return pl.pallas_call(
        project_kernel,
        out_shape=jax.ShapeDtypeStruct((TOK, TOK), bf16),
        in_specs=[VMEM, VMEM],
        out_specs=VMEM,
        scratch_shapes=[
            pltpu.VMEM((4, TOK, TOK), bf16),
            pltpu.VMEM((TOK, TOK), bf16),
            pltpu.VMEM((3, TOK, TOK), bf16),
            pltpu.VMEM((2, TOK // 2, TOK), bf16),
            pltpu.VMEM((2, TOK, TOK), bf16),
            pltpu.SemaphoreType.DMA((16,)),
            pltpu.SemaphoreType.DMA((16,)),
        ],
        compiler_params=pltpu.CompilerParams(
            vmem_limit_bytes=48 * 2**20, collective_id=1, has_side_effects=True
        ),
    )(attended, o_weight)


def solution(mesh):
    return jax.shard_map(
        local,
        mesh=mesh,
        in_specs=(
            P("ctx", "tp"),
            P(None, "ctx", "tp"),
            P(None, "ctx", "tp"),
            P(),
            P(),
            P(),
            P(),
            P("tp", None),
        ),
        out_specs=P("ctx", "tp"),
        check_vma=False,
    )
```

```python
import math

import jax
import jax.numpy as jnp
from jax import lax
from jax.experimental import pallas as pl
from jax.experimental.pallas import tpu as pltpu
from jax.sharding import PartitionSpec as P

QH = 32
KVH = 8
HD = 128
BLK = 128
NG = 16
NS = 4
TOK = 512
PREFIX_BLOCKS = 512
CHUNKS = TOK // BLK
HEADS = QH // KVH
ROWS = HEADS * BLK
WINDOW = 16
REACH = 13
X_SIZE = 4
Z_SIZE = 8
Y_SIZE = 4
QUARTER = NG * BLK // X_SIZE
HALF = QUARTER // 2
PIECE = QUARTER // Z_SIZE
PREFIX_DEV = 16
FRESH_DEV = 4
COPIES = 80
LOADS = 14
OFF = -1e30
EXP_SCALE = math.log2(math.e) / math.sqrt(HD)
OPEN, SHUT, CAUSAL, FIRST_BAND = 0, 1, 2, 3
BIAS_TILES = FIRST_BAND + HEADS * REACH
MESH = pl.DeviceIdType.MESH
BF16 = jnp.bfloat16
F32 = jnp.float32
TRANSPOSED = (((1,), (1,)), ((), ()))


class Sends:
    def __init__(self, send_sem, recv_sem):
        self.send_sem, self.recv_sem, self.started = send_sem, recv_sem, []

    def start(self, src, dst, device):
        slot = len(self.started)
        copy = pltpu.make_async_remote_copy(
            src_ref=src,
            dst_ref=dst,
            send_sem=self.send_sem.at[slot],
            recv_sem=self.recv_sem.at[slot],
            device_id=device,
            device_id_type=MESH,
        )
        copy.start()
        self.started.append(copy)
        return copy

    def finish(self):
        for copy in self.started:
            copy.wait_send()


def make_bias(starts, widths, first_head, bias):
    rows = lax.broadcasted_iota(jnp.int32, (BLK, BLK), 0)
    cols = lax.broadcasted_iota(jnp.int32, (BLK, BLK), 1)
    bias[OPEN] = jnp.zeros((BLK, BLK), F32)
    bias[SHUT] = jnp.full((BLK, BLK), OFF, F32)
    bias[CAUSAL] = jnp.where(rows >= cols, 0.0, OFF)

    @pl.loop(0, HEADS)
    def per_head(head):
        @pl.loop(0, REACH)
        def per_tile(tile):
            distance = (rows - cols) + tile * BLK
            inside = jnp.zeros((BLK, BLK), jnp.bool_)
            for band in range(NS):
                start = starts[first_head + head, band]
                width = widths[first_head + head, band]
                inside = inside | ((distance >= start) & (distance < start + width))
            bias[FIRST_BAND + head * REACH + tile] = jnp.where(inside, 0.0, OFF)


def make_index(blocks, picks, ctx, tp, index):
    first_own = PREFIX_BLOCKS + ctx * CHUNKS

    @pl.loop(0, HEADS)
    def per_head(head):
        picked = [picks[tp * HEADS + head, slot] == 1 for slot in range(NG)]
        listed = [blocks[tp, slot] for slot in range(NG)]

        @pl.loop(0, CHUNKS)
        def vertical(chunk):
            own = first_own + chunk
            for slot in range(NG):
                seen = jnp.where(listed[slot] < own, OPEN, jnp.where(listed[slot] == own, CAUSAL, SHUT))
                index[chunk, head, slot] = jnp.where(picked[slot], seen, SHUT)

        @pl.loop(0, WINDOW)
        def window(tile):
            block = first_own + tile - (REACH - 1)
            shut = block < PREFIX_BLOCKS
            for slot in range(NG):
                shut = shut | (picked[slot] & (listed[slot] == block))
            for chunk in range(CHUNKS):
                back = chunk + (REACH - 1) - tile
                outside = shut | (back < 0) | (back >= REACH)
                index[chunk, head, NG + tile] = jnp.where(outside, SHUT, FIRST_BAND + head * REACH + back)


def kernel(
    blocks, picks, starts, widths, q_hbm, prefix_hbm, fresh_hbm, w_hbm, out,
    kv_k, kv_v, win, q, w, w_in, mine, far_in, near_in, piece_in, vert, bias, index,
    m_s, l_s, acc_s, s_s, p_s, att, att_in, terms, kept, own_s, far_y, near_y,
    load_sem, send_sem, recv_sem,
):
    ctx = lax.axis_index("ctx")
    tp = lax.axis_index("tp")
    x, z = ctx // Z_SIZE, ctx % Z_SIZE
    y, core = tp // 2, tp % 2
    x_far, x_right, x_left = (x + 2) % X_SIZE, (x + 1) % X_SIZE, (x + 3) % X_SIZE
    y_far, y_right, y_left = (y + 2) % Y_SIZE, (y + 1) % Y_SIZE, (y + 3) % Y_SIZE
    right = (x_right * Z_SIZE + z, tp)
    left = (x_left * Z_SIZE + z, tp)
    along = [(x * Z_SIZE + (z + k) % Z_SIZE, tp) for k in range(1, Z_SIZE)]
    size = X_SIZE * Z_SIZE
    after = ((ctx + 1) % size, tp)
    before = ((ctx + size - 1) % size, tp)
    pair = (ctx, y * 2 + (1 - core))
    up = (ctx, y_right * 2 + core)
    down = (ctx, y_left * 2 + core)
    barrier = pltpu.get_barrier_semaphore()
    partners = [right, left] + along + [after, before, pair, up, down]
    for device in partners:
        pl.semaphore_signal(barrier, inc=1, device_id=device, device_id_type=MESH)

    kv = (kv_k, kv_v)
    loads = []

    def load(src, dst):
        copy = pltpu.make_async_copy(src, dst, load_sem.at[len(loads)])
        copy.start()
        loads.append(copy)
        return copy

    kv_loads = [
        (
            load(prefix_hbm.at[part], kv[part].at[pl.ds(0, PREFIX_DEV)]),
            load(fresh_hbm.at[part], kv[part].at[pl.ds(PREFIX_DEV, FRESH_DEV)]),
        )
        for part in range(2)
    ]
    win_loads = [load(fresh_hbm.at[part], win.at[part, pl.ds(WINDOW - FRESH_DEV, FRESH_DEV)]) for part in range(2)]
    q_load = load(q_hbm, q)
    w_load = load(w_hbm, w)
    sends = Sends(send_sem, recv_sem)

    def rows(start, count):
        return pl.ds(pl.multiple_of(start, PIECE), count)

    def pick(part, quarter):
        for step in range(NG // X_SIZE):
            slot = quarter * (NG // X_SIZE) + step
            block = blocks[tp, slot]
            at_prefix = block - ctx * PREFIX_DEV
            at_fresh = block - PREFIX_BLOCKS - ctx * FRESH_DEV
            in_prefix = (at_prefix >= 0) & (at_prefix < PREFIX_DEV)
            in_fresh = (at_fresh >= 0) & (at_fresh < FRESH_DEV)
            row = jnp.where(in_prefix, at_prefix, jnp.where(in_fresh, PREFIX_DEV + at_fresh, 0))
            value = kv[part][row]
            mine[part, rows(slot * BLK, BLK), :] = jnp.where(in_prefix | in_fresh, value, jnp.zeros_like(value))

    def hand_on(part, age):
        src = WINDOW - FRESH_DEV * (1 + age)
        return sends.start(
            win.at[part, pl.ds(src, FRESH_DEV)], win.at[part, pl.ds(src - FRESH_DEV, FRESH_DEV)], after
        )

    far, near, window, pieces, gathered, spread, relayed = {}, {}, {}, {}, {}, {}, {}
    for part in range(2):
        for copy in kv_loads[part]:
            copy.wait()
        pick(part, x_far)
        if part == 0:
            pl.semaphore_wait(barrier, len(partners))
        far[part] = [
            sends.start(mine.at[part, rows(x_far * QUARTER, HALF), :], far_in.at[part, 0], right),
            sends.start(mine.at[part, rows(x_far * QUARTER + HALF, HALF), :], far_in.at[part, 1], left),
        ]
        pick(part, x_right)
        near[part] = [
            sends.start(
                mine.at[part, rows(x_right * QUARTER + HALF, HALF), :], near_in.at[part, 0, pl.ds(HALF, HALF), :], right
            )
        ]
        pick(part, x_left)
        near[part].append(
            sends.start(mine.at[part, rows(x_left * QUARTER, HALF), :], near_in.at[part, 1, pl.ds(0, HALF), :], left)
        )
        win_loads[part].wait()
        window[part, 0] = hand_on(part, 0)
        pick(part, x)
    weights = [
        sends.start(w_hbm.at[:, pl.ds(pl.multiple_of((to * 2 + 1 - core) * TOK, TOK), TOK)], w_in.at[to], pair)
        for to in range(Y_SIZE)
    ]
    make_bias(starts, widths, tp * HEADS, bias)

    def relay_x(part):
        far[part][0].wait_recv()
        mine[part, rows(x_right * QUARTER, HALF), :] += far_in[part, 0]
        near[part].append(
            sends.start(mine.at[part, rows(x_right * QUARTER, HALF), :], near_in.at[part, 0, pl.ds(0, HALF), :], right)
        )
        far[part][1].wait_recv()
        mine[part, rows(x_left * QUARTER + HALF, HALF), :] += far_in[part, 1]
        near[part].append(
            sends.start(
                mine.at[part, rows(x_left * QUARTER + HALF, HALF), :], near_in.at[part, 1, pl.ds(HALF, HALF), :], left
            )
        )

    def scatter_z(part):
        for copy in near[part]:
            copy.wait_recv()
        own = rows(x * QUARTER, QUARTER)
        mine[part, own, :] = mine[part, own, :] + near_in[part, 0] + near_in[part, 1]
        pieces[part] = [
            sends.start(
                mine.at[part, rows(x * QUARTER + (z + k) % Z_SIZE * PIECE, PIECE), :],
                piece_in.at[part, k - 1],
                along[k - 1],
            )
            for k in range(1, Z_SIZE)
        ]

    def gather_z(part):
        at = rows(x * QUARTER + z * PIECE, PIECE)
        total = mine[part, at, :]
        for k in range(1, Z_SIZE):
            pieces[part][k - 1].wait_recv()
            total = total + piece_in[part, k - 1]
        vert[part, at, :] = total
        gathered[part] = [
            sends.start(vert.at[part, at, :], vert.at[part, at, :], along[k - 1]) for k in range(1, Z_SIZE)
        ]

    def spread_x(part):
        for copy in gathered[part]:
            copy.wait_recv()
        spread[part] = []
        for start in (0, HALF):
            at = rows(x * QUARTER + start, HALF)
            for device in (right, left):
                spread[part].append(sends.start(vert.at[part, at, :], vert.at[part, at, :], device))

    def relay_back(part):
        top_right, top_left, low_right, low_left = spread[part]
        top_right.wait_recv()
        at = rows(x_left * QUARTER, HALF)
        relayed[part] = [sends.start(vert.at[part, at, :], vert.at[part, at, :], right)]
        low_left.wait_recv()
        at = rows(x_right * QUARTER + HALF, HALF)
        relayed[part].append(sends.start(vert.at[part, at, :], vert.at[part, at, :], left))

    def complete(part):
        spread[part][1].wait_recv()
        spread[part][2].wait_recv()
        for copy in relayed[part]:
            copy.wait_recv()

    def pass_window(age):
        for part in range(2):
            window[part, age].wait_recv()
            if age < 2:
                window[part, age + 1] = hand_on(part, age + 1)

    def queries(chunk, head):
        return q[pl.ds(pl.multiple_of(chunk * BLK, BLK), BLK), head * HD : (head + 1) * HD]

    def head_rows(head):
        return slice(head * BLK, (head + 1) * BLK)

    def score(chunk, head, keys, tile, column, count, best):
        s = lax.dot_general(queries(chunk, head), keys, TRANSPOSED, preferred_element_type=F32)
        for j in range(count):
            piece = s[:, j * BLK : (j + 1) * BLK] + bias[index[chunk, head, tile + j]]
            s_s[head_rows(head), (column + j) * BLK : (column + j + 1) * BLK] = piece
            best = piece if best is None else jnp.maximum(best, piece)
        return best

    def weigh(head, top, column, count, total):
        probs = []
        for j in range(count):
            piece = s_s[head_rows(head), (column + j) * BLK : (column + j + 1) * BLK]
            piece = jnp.exp2((piece - top) * EXP_SCALE)
            total = piece if total is None else total + piece
            probs.append(piece.astype(BF16))
        return jnp.concatenate(probs, axis=1), total

    def wide(best):
        return jnp.broadcast_to(jnp.max(best, axis=1, keepdims=True), (BLK, BLK))

    def band(chunks, first, count, begin):
        @pl.loop(*chunks)
        def per_chunk(chunk):
            keys = win[0, first : first + count].reshape(count * BLK, HD)
            values = win[1, first : first + count].reshape(count * BLK, HD)
            best = None
            for head in range(HEADS + 1):
                fresh = None
                if head < HEADS:
                    fresh = score(chunk, head, keys, NG + first, 0, count, None)
                if head > 0:
                    done = head_rows(head - 1)
                    top = wide(best)
                    if not begin:
                        top = jnp.maximum(m_s[chunk, done, :], top)
                    probs, total = weigh(head - 1, top, 0, count, None)
                    product = jnp.dot(probs, values, preferred_element_type=F32)
                    if begin:
                        l_s[chunk, done, :] = total
                        acc_s[chunk, done, :] = product
                    else:
                        fade = jnp.exp2((m_s[chunk, done, :] - top) * EXP_SCALE)
                        l_s[chunk, done, :] = l_s[chunk, done, :] * fade + total
                        acc_s[chunk, done, :] = acc_s[chunk, done, :] * fade + product
                    m_s[chunk, done, :] = top
                best = fresh

    def vertical_scores(chunks):
        step = NG // 2

        @pl.loop(*chunks)
        def per_chunk(chunk):
            best = None
            for head in range(HEADS + 1):
                if head > 0:
                    done = head_rows(head - 1)
                    top = jnp.maximum(m_s[chunk, done, :], wide(best))
                    fade = jnp.exp2((m_s[chunk, done, :] - top) * EXP_SCALE)
                    total = l_s[chunk, done, :] * fade
                best = None
                for first in (0, step):
                    if head < HEADS:
                        keys = vert[0, first * BLK : (first + step) * BLK, :]
                        best = score(chunk, head, keys, first, first, step, best)
                    if head > 0:
                        probs, total = weigh(head - 1, top, first, step, total)
                        p_s[chunk, done, first * BLK : (first + step) * BLK] = probs
                if head > 0:
                    acc_s[chunk, done, :] = acc_s[chunk, done, :] * fade
                    l_s[chunk, done, :] = total

    def vertical_values(chunks):
        @pl.loop(*chunks)
        def per_chunk(chunk):
            product = jnp.dot(p_s[chunk], vert[1], preferred_element_type=F32)
            result = (acc_s[chunk] + product) / jnp.sum(l_s[chunk], axis=1, keepdims=True)
            for head in range(HEADS):
                att[pl.ds(pl.multiple_of(chunk * BLK, BLK), BLK), head * HD : (head + 1) * HD] = result[
                    head_rows(head), :
                ].astype(BF16)

    span = TOK // 2
    part_rows = span // 2

    def exchange(half):
        at = pl.ds(half * span, span)
        return sends.start(att.at[at, :], att_in.at[at, :], pair)

    def term(half, to):
        columns = pl.ds(pl.multiple_of((to * 2 + core) * TOK, TOK), TOK)
        at = slice(half * span, (half + 1) * span)
        total = jnp.dot(att[at, :], w[:, columns], preferred_element_type=F32)
        return total + jnp.dot(att_in[at, :], w_in[to], preferred_element_type=F32)

    def cut(half):
        start = half * span
        return pl.ds(start, part_rows), pl.ds(start + part_rows, part_rows)

    far_sum, near_sum = {}, {}

    def project(half):
        top, low = cut(half)
        total = term(half, y_far)
        terms[0, top, :] = total[:part_rows].astype(BF16)
        terms[0, low, :] = total[part_rows:].astype(BF16)
        far_sum[half] = [
            sends.start(terms.at[0, top, :], far_y.at[half, 0], up),
            sends.start(terms.at[0, low, :], far_y.at[half, 1], down),
        ]
        total = term(half, y_right)
        terms[1, low, :] = total[part_rows:].astype(BF16)
        kept[half, 0] = total[:part_rows]
        near_sum[half] = [sends.start(terms.at[1, low, :], near_y.at[0, low, :], up)]
        total = term(half, y_left)
        terms[2, top, :] = total[:part_rows].astype(BF16)
        kept[half, 1] = total[part_rows:]
        near_sum[half].append(sends.start(terms.at[2, top, :], near_y.at[1, top, :], down))

    def project_own(half):
        own_s[half] = term(half, y)

    def relay_y(half):
        top, low = cut(half)
        far_sum[half][0].wait_recv()
        terms[1, top, :] = (kept[half, 0] + far_y[half, 0].astype(F32)).astype(BF16)
        near_sum[half].append(sends.start(terms.at[1, top, :], near_y.at[0, top, :], up))
        far_sum[half][1].wait_recv()
        terms[2, low, :] = (kept[half, 1] + far_y[half, 1].astype(F32)).astype(BF16)
        near_sum[half].append(sends.start(terms.at[2, low, :], near_y.at[1, low, :], down))

    def total_up(half):
        for copy in near_sum[half]:
            copy.wait_recv()
        at = slice(half * span, (half + 1) * span)
        out[at, :] = (own_s[half] + near_y[0, at, :].astype(F32) + near_y[1, at, :].astype(F32)).astype(BF16)

    relay_x(0)
    make_index(blocks, picks, ctx, tp, index)
    relay_x(1)
    scatter_z(0)
    q_load.wait()
    pass_window(0)
    band((0, 2), 8, 8, True)
    scatter_z(1)
    band((2, 4), 8, 8, True)
    gather_z(0)
    pass_window(1)
    gather_z(1)
    band((0, 4), 4, 4, False)
    spread_x(0)
    spread_x(1)
    relay_back(0)
    pass_window(2)
    band((0, 4), 0, 4, False)
    relay_back(1)
    complete(0)
    vertical_scores((0, 4))
    complete(1)
    vertical_values((0, 2))
    first = exchange(0)
    vertical_values((2, 4))
    second = exchange(1)
    w_load.wait()
    for copy in weights:
        copy.wait_recv()
    first.wait_recv()
    project(0)
    second.wait_recv()
    project(1)
    relay_y(0)
    project_own(0)
    relay_y(1)
    project_own(1)
    total_up(0)
    total_up(1)
    sends.finish()


def local(queries, prefix_kv, fresh_kv, group_blocks, head_pick, band_start, band_width, o_weight):
    vmem = pl.BlockSpec(memory_space=pltpu.VMEM)
    smem = pl.BlockSpec(memory_space=pltpu.SMEM)
    hbm = pl.BlockSpec(memory_space=pl.ANY)
    return pl.pallas_call(
        kernel,
        out_shape=jax.ShapeDtypeStruct((TOK, TOK), BF16),
        in_specs=[smem] * 4 + [hbm] * 4,
        out_specs=vmem,
        scratch_shapes=[
            pltpu.VMEM((PREFIX_DEV + FRESH_DEV, BLK, HD), BF16),
            pltpu.VMEM((PREFIX_DEV + FRESH_DEV, BLK, HD), BF16),
            pltpu.VMEM((2, WINDOW, BLK, HD), BF16),
            pltpu.VMEM((TOK, HEADS * HD), BF16),
            pltpu.VMEM((TOK, QH * HD), BF16),
            pltpu.VMEM((Y_SIZE, TOK, TOK), BF16),
            pltpu.VMEM((2, NG * BLK, HD), BF16),
            pltpu.VMEM((2, 2, HALF, HD), BF16),
            pltpu.VMEM((2, 2, QUARTER, HD), BF16),
            pltpu.VMEM((2, Z_SIZE - 1, PIECE, HD), BF16),
            pltpu.VMEM((2, NG * BLK, HD), BF16),
            pltpu.VMEM((BIAS_TILES, BLK, BLK), F32),
            pltpu.SMEM((CHUNKS, HEADS, NG + WINDOW), jnp.int32),
            pltpu.VMEM((CHUNKS, ROWS, BLK), F32),
            pltpu.VMEM((CHUNKS, ROWS, BLK), F32),
            pltpu.VMEM((CHUNKS, ROWS, HD), F32),
            pltpu.VMEM((ROWS, NG * BLK), F32),
            pltpu.VMEM((CHUNKS, ROWS, NG * BLK), BF16),
            pltpu.VMEM((TOK, HEADS * HD), BF16),
            pltpu.VMEM((TOK, HEADS * HD), BF16),
            pltpu.VMEM((3, TOK, TOK), BF16),
            pltpu.VMEM((2, 2, TOK // 4, TOK), F32),
            pltpu.VMEM((2, TOK // 2, TOK), F32),
            pltpu.VMEM((2, 2, TOK // 4, TOK), BF16),
            pltpu.VMEM((2, TOK, TOK), BF16),
            pltpu.SemaphoreType.DMA((LOADS,)),
            pltpu.SemaphoreType.DMA((COPIES,)),
            pltpu.SemaphoreType.DMA((COPIES,)),
        ],
        compiler_params=pltpu.CompilerParams(
            vmem_limit_bytes=56 * 2**20, collective_id=0, has_side_effects=True
        ),
    )(
        group_blocks,
        head_pick,
        band_start,
        band_width,
        queries,
        prefix_kv.reshape(2, PREFIX_DEV, BLK, HD),
        fresh_kv.reshape(2, FRESH_DEV, BLK, HD),
        o_weight,
    )


def solution(mesh):
    return jax.shard_map(
        local,
        mesh=mesh,
        in_specs=(
            P("ctx", "tp"),
            P(None, "ctx", "tp"),
            P(None, "ctx", "tp"),
            P(),
            P(),
            P(),
            P(),
            P("tp", None),
        ),
        out_specs=P("ctx", "tp"),
        check_vma=False,
    )
```

```python
import math

import jax
import jax.numpy as jnp
from jax import lax
from jax.experimental import pallas as pl
from jax.experimental.pallas import tpu as pltpu
from jax.sharding import PartitionSpec as P

QH = 32
KVH = 8
HD = 128
BLK = 128
NG = 16
NS = 4
TOK = 512
PREFIX_BLOCKS = 512
CHUNKS = TOK // BLK
HEADS = QH // KVH
ROWS = HEADS * BLK
WINDOW = 16
REACH = 13
X_SIZE = 4
Z_SIZE = 8
Y_SIZE = 4
QUARTER = NG * BLK // X_SIZE
HALF = QUARTER // 2
PIECE = QUARTER // Z_SIZE
PREFIX_DEV = 16
FRESH_DEV = 4
COPIES = 80
WRAP_COLUMN = 0
LOADS = 14
OFF = -1e30
EXP_SCALE = math.log2(math.e) / math.sqrt(HD)
OPEN, SHUT, CAUSAL, FIRST_BAND = 0, 1, 2, 3
BIAS_TILES = FIRST_BAND + HEADS * REACH
MESH = pl.DeviceIdType.MESH
BF16 = jnp.bfloat16
F32 = jnp.float32
TRANSPOSED = (((1,), (1,)), ((), ()))


class Sends:
    def __init__(self, send_sem, recv_sem):
        self.send_sem, self.recv_sem, self.started = send_sem, recv_sem, []

    def start(self, src, dst, device):
        slot = len(self.started)
        copy = pltpu.make_async_remote_copy(
            src_ref=src,
            dst_ref=dst,
            send_sem=self.send_sem.at[slot],
            recv_sem=self.recv_sem.at[slot],
            device_id=device,
            device_id_type=MESH,
        )
        copy.start()
        self.started.append(copy)
        return copy

    def finish(self):
        for copy in self.started:
            copy.wait_send()


def make_bias(starts, widths, first_head, bias):
    rows = lax.broadcasted_iota(jnp.int32, (BLK, BLK), 0)
    cols = lax.broadcasted_iota(jnp.int32, (BLK, BLK), 1)
    bias[OPEN] = jnp.zeros((BLK, BLK), F32)
    bias[SHUT] = jnp.full((BLK, BLK), OFF, F32)
    bias[CAUSAL] = jnp.where(rows >= cols, 0.0, OFF)

    @pl.loop(0, HEADS)
    def per_head(head):
        @pl.loop(0, REACH)
        def per_tile(tile):
            distance = (rows - cols) + tile * BLK
            inside = jnp.zeros((BLK, BLK), jnp.bool_)
            for band in range(NS):
                start = starts[band, first_head + head]
                width = widths[band, first_head + head]
                inside = inside | ((distance >= start) & (distance < start + width))
            bias[FIRST_BAND + head * REACH + tile] = jnp.where(inside, 0.0, OFF)


def make_index(blocks, picks, ctx, tp, index):
    first_own = PREFIX_BLOCKS + ctx * CHUNKS

    @pl.loop(0, HEADS)
    def per_head(head):
        picked = [picks[slot, tp * HEADS + head] == 1 for slot in range(NG)]
        listed = [blocks[tp, slot] for slot in range(NG)]

        @pl.loop(0, CHUNKS)
        def vertical(chunk):
            own = first_own + chunk
            for slot in range(NG):
                seen = jnp.where(listed[slot] < own, OPEN, jnp.where(listed[slot] == own, CAUSAL, SHUT))
                index[chunk, head, slot] = jnp.where(picked[slot], seen, SHUT)

        @pl.loop(0, WINDOW)
        def window(tile):
            block = first_own + tile - (REACH - 1)
            shut = block < PREFIX_BLOCKS
            for slot in range(NG):
                shut = shut | (picked[slot] & (listed[slot] == block))
            for chunk in range(CHUNKS):
                back = chunk + (REACH - 1) - tile
                outside = shut | (back < 0) | (back >= REACH)
                index[chunk, head, NG + tile] = jnp.where(outside, SHUT, FIRST_BAND + head * REACH + back)


def kernel(
    blocks, picks, starts, widths, q_hbm, prefix_hbm, fresh_hbm, w_hbm, out,
    kv_k, kv_v, win, q, w, w_in, mine, far_in, near_in, piece_in, vert, bias, index,
    m_s, l_s, acc_s, s_s, p_s, att, att_in, terms, kept, own_s, far_y, near_y,
    load_sem, send_sem, recv_sem,
):
    ctx = lax.axis_index("ctx")
    tp = lax.axis_index("tp")
    x, z = ctx // Z_SIZE, ctx % Z_SIZE
    y, core = tp // 2, tp % 2
    x_far, x_right, x_left = (x + 2) % X_SIZE, (x + 1) % X_SIZE, (x + 3) % X_SIZE
    y_far, y_right, y_left = (y + 2) % Y_SIZE, (y + 1) % Y_SIZE, (y + 3) % Y_SIZE
    turned = z == WRAP_COLUMN
    x_a = jnp.where(turned, x_left, x_right)
    x_b = jnp.where(turned, x_right, x_left)
    side_a = (x_a * Z_SIZE + z, tp)
    side_b = (x_b * Z_SIZE + z, tp)
    right = (x_right * Z_SIZE + z, tp)
    left = (x_left * Z_SIZE + z, tp)
    along = [(x * Z_SIZE + (z + k) % Z_SIZE, tp) for k in range(1, Z_SIZE)]
    size = X_SIZE * Z_SIZE
    after = ((ctx + 1) % size, tp)
    before = ((ctx + size - 1) % size, tp)
    pair = (ctx, y * 2 + (1 - core))
    up = (ctx, y_right * 2 + core)
    down = (ctx, y_left * 2 + core)
    barrier = pltpu.get_barrier_semaphore()
    partners = [right, left] + along + [after, before, pair, up, down]
    for device in partners:
        pl.semaphore_signal(barrier, inc=1, device_id=device, device_id_type=MESH)

    kv = (kv_k, kv_v)
    loads = []

    def load(src, dst):
        copy = pltpu.make_async_copy(src, dst, load_sem.at[len(loads)])
        copy.start()
        loads.append(copy)
        return copy

    kv_loads = [
        (
            load(prefix_hbm.at[part], kv[part].at[pl.ds(0, PREFIX_DEV)]),
            load(fresh_hbm.at[part], kv[part].at[pl.ds(PREFIX_DEV, FRESH_DEV)]),
        )
        for part in range(2)
    ]
    win_loads = [load(fresh_hbm.at[part], win.at[part, pl.ds(WINDOW - FRESH_DEV, FRESH_DEV)]) for part in range(2)]
    q_load = load(q_hbm, q)
    w_load = load(w_hbm, w)
    sends = Sends(send_sem, recv_sem)

    def rows(start, count):
        return pl.ds(pl.multiple_of(start, PIECE), count)

    def pick(part, quarter):
        for step in range(NG // X_SIZE):
            slot = quarter * (NG // X_SIZE) + step
            block = blocks[tp, slot]
            at_prefix = block - ctx * PREFIX_DEV
            at_fresh = block - PREFIX_BLOCKS - ctx * FRESH_DEV
            in_prefix = (at_prefix >= 0) & (at_prefix < PREFIX_DEV)
            in_fresh = (at_fresh >= 0) & (at_fresh < FRESH_DEV)
            row = jnp.where(in_prefix, at_prefix, jnp.where(in_fresh, PREFIX_DEV + at_fresh, 0))
            value = kv[part][row]
            mine[part, rows(slot * BLK, BLK), :] = jnp.where(in_prefix | in_fresh, value, jnp.zeros_like(value))

    def hand_on(part, age):
        src = WINDOW - FRESH_DEV * (1 + age)
        return sends.start(
            win.at[part, pl.ds(src, FRESH_DEV)], win.at[part, pl.ds(src - FRESH_DEV, FRESH_DEV)], after
        )

    far, near, window, pieces, gathered, spread, relayed = {}, {}, {}, {}, {}, {}, {}
    def far_start(part):
        far[part] = [
            sends.start(mine.at[part, rows(x_far * QUARTER, HALF), :], far_in.at[part, 0], side_a),
            sends.start(mine.at[part, rows(x_far * QUARTER + HALF, HALF), :], far_in.at[part, 1], left),
        ]

    def near_start(part):
        pick(part, x_right)
        pick(part, x_left)
        near[part] = [
            sends.start(mine.at[part, rows(x_b * QUARTER, HALF), :], near_in.at[part, 1, pl.ds(0, HALF), :], side_b),
            sends.start(
                mine.at[part, rows(x_right * QUARTER + HALF, HALF), :], near_in.at[part, 0, pl.ds(HALF, HALF), :], right
            ),
        ]

    def relay_x(part):
        far[part][0].wait_recv()
        mine[part, rows(x_a * QUARTER, HALF), :] += far_in[part, 0]
        near[part].append(
            sends.start(mine.at[part, rows(x_a * QUARTER, HALF), :], near_in.at[part, 0, pl.ds(0, HALF), :], side_a)
        )
        far[part][1].wait_recv()
        mine[part, rows(x_left * QUARTER + HALF, HALF), :] += far_in[part, 1]
        near[part].append(
            sends.start(
                mine.at[part, rows(x_left * QUARTER + HALF, HALF), :], near_in.at[part, 1, pl.ds(HALF, HALF), :], left
            )
        )

    def start_window():
        for part in range(2):
            win_loads[part].wait()
            window[part, 0] = hand_on(part, 0)

    def scatter_z(part):
        for copy in near[part]:
            copy.wait_recv()
        own = rows(x * QUARTER, QUARTER)
        mine[part, own, :] = mine[part, own, :] + near_in[part, 0] + near_in[part, 1]
        pieces[part] = [
            sends.start(
                mine.at[part, rows(x * QUARTER + (z + k) % Z_SIZE * PIECE, PIECE), :],
                piece_in.at[part, k - 1],
                along[k - 1],
            )
            for k in range(1, Z_SIZE)
        ]

    def gather_z(part):
        at = rows(x * QUARTER + z * PIECE, PIECE)
        total = mine[part, at, :]
        for k in range(1, Z_SIZE):
            pieces[part][k - 1].wait_recv()
            total = total + piece_in[part, k - 1]
        vert[part, at, :] = total
        gathered[part] = [
            sends.start(vert.at[part, at, :], vert.at[part, at, :], along[k - 1]) for k in range(1, Z_SIZE)
        ]

    def spread_x(part):
        for copy in gathered[part]:
            copy.wait_recv()
        top = rows(x * QUARTER, HALF)
        low = rows(x * QUARTER + HALF, HALF)
        spread[part] = [
            sends.start(vert.at[part, at, :], vert.at[part, at, :], device)
            for at, device in ((top, side_a), (low, left), (top, side_b), (low, right))
        ]

    def relay_back(part):
        spread[part][0].wait_recv()
        at = rows(x_b * QUARTER, HALF)
        relayed[part] = [sends.start(vert.at[part, at, :], vert.at[part, at, :], side_a)]
        spread[part][1].wait_recv()
        at = rows(x_right * QUARTER + HALF, HALF)
        relayed[part].append(sends.start(vert.at[part, at, :], vert.at[part, at, :], left))

    def complete(part):
        spread[part][2].wait_recv()
        spread[part][3].wait_recv()
        for copy in relayed[part]:
            copy.wait_recv()

    def pass_window(age):
        for part in range(2):
            window[part, age].wait_recv()
            if age < 2:
                window[part, age + 1] = hand_on(part, age + 1)

    def queries(chunk, head):
        return q[pl.ds(pl.multiple_of(chunk * BLK, BLK), BLK), head * HD : (head + 1) * HD]

    def head_rows(head):
        return slice(head * BLK, (head + 1) * BLK)

    def score(chunk, head, keys, tile, column, count, best):
        s = lax.dot_general(queries(chunk, head), keys, TRANSPOSED, preferred_element_type=F32)
        for j in range(count):
            piece = s[:, j * BLK : (j + 1) * BLK] + bias[index[chunk, head, tile + j]]
            s_s[head_rows(head), (column + j) * BLK : (column + j + 1) * BLK] = piece
            best = piece if best is None else jnp.maximum(best, piece)
        return best

    def weigh(head, top, column, count, total):
        probs = []
        for j in range(count):
            piece = s_s[head_rows(head), (column + j) * BLK : (column + j + 1) * BLK]
            piece = jnp.exp2((piece - top) * EXP_SCALE)
            total = piece if total is None else total + piece
            probs.append(piece.astype(BF16))
        return jnp.concatenate(probs, axis=1), total

    def wide(best):
        return jnp.broadcast_to(jnp.max(best, axis=1, keepdims=True), (BLK, BLK))

    def band(chunks, first, count, begin):
        @pl.loop(*chunks)
        def per_chunk(chunk):
            keys = win[0, first : first + count].reshape(count * BLK, HD)
            values = win[1, first : first + count].reshape(count * BLK, HD)
            best = None
            for head in range(HEADS + 1):
                fresh = None
                if head < HEADS:
                    fresh = score(chunk, head, keys, NG + first, 0, count, None)
                if head > 0:
                    done = head_rows(head - 1)
                    top = wide(best)
                    if not begin:
                        top = jnp.maximum(m_s[chunk, done, :], top)
                    probs, total = weigh(head - 1, top, 0, count, None)
                    product = jnp.dot(probs, values, preferred_element_type=F32)
                    if begin:
                        l_s[chunk, done, :] = total
                        acc_s[chunk, done, :] = product
                    else:
                        fade = jnp.exp2((m_s[chunk, done, :] - top) * EXP_SCALE)
                        l_s[chunk, done, :] = l_s[chunk, done, :] * fade + total
                        acc_s[chunk, done, :] = acc_s[chunk, done, :] * fade + product
                    m_s[chunk, done, :] = top
                best = fresh

    def vertical_scores(chunks):
        step = NG // 2

        @pl.loop(*chunks)
        def per_chunk(chunk):
            best = None
            for head in range(HEADS + 1):
                if head > 0:
                    done = head_rows(head - 1)
                    top = jnp.maximum(m_s[chunk, done, :], wide(best))
                    fade = jnp.exp2((m_s[chunk, done, :] - top) * EXP_SCALE)
                    total = l_s[chunk, done, :] * fade
                best = None
                for first in (0, step):
                    if head < HEADS:
                        keys = vert[0, first * BLK : (first + step) * BLK, :]
                        best = score(chunk, head, keys, first, first, step, best)
                    if head > 0:
                        probs, total = weigh(head - 1, top, first, step, total)
                        p_s[chunk, done, first * BLK : (first + step) * BLK] = probs
                if head > 0:
                    acc_s[chunk, done, :] = acc_s[chunk, done, :] * fade
                    l_s[chunk, done, :] = total

    def vertical_values(chunks):
        @pl.loop(*chunks)
        def per_chunk(chunk):
            product = jnp.dot(p_s[chunk], vert[1], preferred_element_type=F32)
            result = (acc_s[chunk] + product) / jnp.sum(l_s[chunk], axis=1, keepdims=True)
            for head in range(HEADS):
                att[pl.ds(pl.multiple_of(chunk * BLK, BLK), BLK), head * HD : (head + 1) * HD] = result[
                    head_rows(head), :
                ].astype(BF16)

    span = TOK // 2
    part_rows = span // 2

    def exchange(half):
        at = pl.ds(half * span, span)
        return sends.start(att.at[at, :], att_in.at[at, :], pair)

    def term(half, to):
        columns = pl.ds(pl.multiple_of((to * 2 + core) * TOK, TOK), TOK)
        at = slice(half * span, (half + 1) * span)
        total = jnp.dot(att[at, :], w[:, columns], preferred_element_type=F32)
        return total + jnp.dot(att_in[at, :], w_in[to], preferred_element_type=F32)

    def cut(half):
        start = half * span
        return pl.ds(start, part_rows), pl.ds(start + part_rows, part_rows)

    far_sum, near_sum = {}, {}

    def project(half):
        top, low = cut(half)
        total = term(half, y_far)
        terms[0, top, :] = total[:part_rows].astype(BF16)
        terms[0, low, :] = total[part_rows:].astype(BF16)
        far_sum[half] = [
            sends.start(terms.at[0, top, :], far_y.at[half, 0], up),
            sends.start(terms.at[0, low, :], far_y.at[half, 1], down),
        ]
        total = term(half, y_right)
        terms[1, low, :] = total[part_rows:].astype(BF16)
        kept[half, 0] = total[:part_rows]
        near_sum[half] = [sends.start(terms.at[1, low, :], near_y.at[0, low, :], up)]
        total = term(half, y_left)
        terms[2, top, :] = total[:part_rows].astype(BF16)
        kept[half, 1] = total[part_rows:]
        near_sum[half].append(sends.start(terms.at[2, top, :], near_y.at[1, top, :], down))

    def project_own(half):
        own_s[half] = term(half, y)

    def relay_y(half):
        top, low = cut(half)
        far_sum[half][0].wait_recv()
        terms[1, top, :] = (kept[half, 0] + far_y[half, 0].astype(F32)).astype(BF16)
        near_sum[half].append(sends.start(terms.at[1, top, :], near_y.at[0, top, :], up))
        far_sum[half][1].wait_recv()
        terms[2, low, :] = (kept[half, 1] + far_y[half, 1].astype(F32)).astype(BF16)
        near_sum[half].append(sends.start(terms.at[2, low, :], near_y.at[1, low, :], down))

    def total_up(half):
        for copy in near_sum[half]:
            copy.wait_recv()
        at = slice(half * span, (half + 1) * span)
        out[at, :] = (own_s[half] + near_y[0, at, :].astype(F32) + near_y[1, at, :].astype(F32)).astype(BF16)

    weights = []

    def start_weights():
        for to in range(Y_SIZE):
            columns = pl.ds(pl.multiple_of((to * 2 + 1 - core) * TOK, TOK), TOK)
            weights.append(sends.start(w_hbm.at[:, columns], w_in.at[to], pair))

    for copy in kv_loads[0]:
        copy.wait()
    pick(0, x_far)
    pl.semaphore_wait(barrier, len(partners))
    far_start(0)
    near_start(0)
    for copy in kv_loads[1]:
        copy.wait()
    pick(1, x_far)
    far_start(1)
    start_window()
    pick(0, x)
    relay_x(0)
    near_start(1)
    pick(1, x)
    relay_x(1)
    start_weights()
    make_bias(starts, widths, tp * HEADS, bias)
    scatter_z(0)
    make_index(blocks, picks, ctx, tp, index)
    q_load.wait()
    scatter_z(1)
    pass_window(0)
    band((0, 2), 8, 8, True)
    gather_z(0)
    band((2, 3), 8, 8, True)
    gather_z(1)
    pass_window(1)
    band((3, 4), 8, 8, True)
    band((0, 2), 4, 4, False)
    spread_x(0)
    band((2, 4), 4, 4, False)
    spread_x(1)
    relay_back(0)
    pass_window(2)
    relay_back(1)
    band((0, 4), 0, 4, False)
    complete(0)
    vertical_scores((0, 4))
    complete(1)
    vertical_values((0, 2))
    first = exchange(0)
    vertical_values((2, 4))
    second = exchange(1)
    w_load.wait()
    for copy in weights:
        copy.wait_recv()
    first.wait_recv()
    project(0)
    second.wait_recv()
    project(1)
    relay_y(0)
    project_own(0)
    relay_y(1)
    project_own(1)
    total_up(0)
    total_up(1)
    sends.finish()


def local(queries, prefix_kv, fresh_kv, group_blocks, head_pick, band_start, band_width, o_weight):
    vmem = pl.BlockSpec(memory_space=pltpu.VMEM)
    smem = pl.BlockSpec(memory_space=pltpu.SMEM)
    hbm = pl.BlockSpec(memory_space=pl.ANY)
    return pl.pallas_call(
        kernel,
        out_shape=jax.ShapeDtypeStruct((TOK, TOK), BF16),
        in_specs=[smem] * 4 + [hbm] * 4,
        out_specs=vmem,
        scratch_shapes=[
            pltpu.VMEM((PREFIX_DEV + FRESH_DEV, BLK, HD), BF16),
            pltpu.VMEM((PREFIX_DEV + FRESH_DEV, BLK, HD), BF16),
            pltpu.VMEM((2, WINDOW, BLK, HD), BF16),
            pltpu.VMEM((TOK, HEADS * HD), BF16),
            pltpu.VMEM((TOK, QH * HD), BF16),
            pltpu.VMEM((Y_SIZE, TOK, TOK), BF16),
            pltpu.VMEM((2, NG * BLK, HD), BF16),
            pltpu.VMEM((2, 2, HALF, HD), BF16),
            pltpu.VMEM((2, 2, QUARTER, HD), BF16),
            pltpu.VMEM((2, Z_SIZE - 1, PIECE, HD), BF16),
            pltpu.VMEM((2, NG * BLK, HD), BF16),
            pltpu.VMEM((BIAS_TILES, BLK, BLK), F32),
            pltpu.SMEM((CHUNKS, HEADS, NG + WINDOW), jnp.int32),
            pltpu.VMEM((CHUNKS, ROWS, BLK), F32),
            pltpu.VMEM((CHUNKS, ROWS, BLK), F32),
            pltpu.VMEM((CHUNKS, ROWS, HD), F32),
            pltpu.VMEM((ROWS, NG * BLK), F32),
            pltpu.VMEM((CHUNKS, ROWS, NG * BLK), BF16),
            pltpu.VMEM((TOK, HEADS * HD), BF16),
            pltpu.VMEM((TOK, HEADS * HD), BF16),
            pltpu.VMEM((3, TOK, TOK), BF16),
            pltpu.VMEM((2, 2, TOK // 4, TOK), F32),
            pltpu.VMEM((2, TOK // 2, TOK), F32),
            pltpu.VMEM((2, 2, TOK // 4, TOK), BF16),
            pltpu.VMEM((2, TOK, TOK), BF16),
            pltpu.SemaphoreType.DMA((LOADS,)),
            pltpu.SemaphoreType.DMA((COPIES,)),
            pltpu.SemaphoreType.DMA((COPIES,)),
        ],
        compiler_params=pltpu.CompilerParams(
            vmem_limit_bytes=56 * 2**20, collective_id=0, has_side_effects=True
        ),
    )(
        group_blocks,
        head_pick.T,
        band_start.T,
        band_width.T,
        queries,
        prefix_kv.reshape(2, PREFIX_DEV, BLK, HD),
        fresh_kv.reshape(2, FRESH_DEV, BLK, HD),
        o_weight,
    )


def solution(mesh):
    return jax.shard_map(
        local,
        mesh=mesh,
        in_specs=(
            P("ctx", "tp"),
            P(None, "ctx", "tp"),
            P(None, "ctx", "tp"),
            P(),
            P(),
            P(),
            P(),
            P("tp", None),
        ),
        out_specs=P("ctx", "tp"),
        check_vma=False,
    )
```

```python
import math

import jax
import jax.numpy as jnp
from jax import lax
from jax.experimental import pallas as pl
from jax.experimental.pallas import tpu as pltpu
from jax.sharding import PartitionSpec as P

QH = 32
KVH = 8
HD = 128
BLK = 128
NG = 16
NS = 4
TOK = 512
PREFIX_BLOCKS = 512
CHUNKS = TOK // BLK
HEADS = QH // KVH
ROWS = HEADS * BLK
WINDOW = 16
REACH = 13
X_SIZE = 4
Z_SIZE = 8
Y_SIZE = 4
QUARTER = NG * BLK // X_SIZE
HALF = QUARTER // 2
PIECE = QUARTER // Z_SIZE
PREFIX_DEV = 16
FRESH_DEV = 4
COPIES = 96
UNITS = 4
WRAP_COLUMN = 0
LOADS = 14
OFF = -1e30
EXP_SCALE = math.log2(math.e) / math.sqrt(HD)
OPEN, SHUT, CAUSAL, FIRST_BAND = 0, 1, 2, 3
BIAS_TILES = FIRST_BAND + HEADS * REACH
MESH = pl.DeviceIdType.MESH
BF16 = jnp.bfloat16
F32 = jnp.float32
TRANSPOSED = (((1,), (1,)), ((), ()))


class Sends:
    def __init__(self, send_sem, recv_sem):
        self.send_sem, self.recv_sem, self.started = send_sem, recv_sem, []

    def start(self, src, dst, device):
        slot = len(self.started)
        copy = pltpu.make_async_remote_copy(
            src_ref=src,
            dst_ref=dst,
            send_sem=self.send_sem.at[slot],
            recv_sem=self.recv_sem.at[slot],
            device_id=device,
            device_id_type=MESH,
        )
        copy.start()
        self.started.append(copy)
        return copy

    def finish(self):
        for copy in self.started:
            copy.wait_send()


def make_bias(starts, widths, first_head, bias):
    rows = lax.broadcasted_iota(jnp.int32, (BLK, BLK), 0)
    cols = lax.broadcasted_iota(jnp.int32, (BLK, BLK), 1)
    bias[OPEN] = jnp.zeros((BLK, BLK), F32)
    bias[SHUT] = jnp.full((BLK, BLK), OFF, F32)
    bias[CAUSAL] = jnp.where(rows >= cols, 0.0, OFF)

    @pl.loop(0, HEADS)
    def per_head(head):
        @pl.loop(0, REACH)
        def per_tile(tile):
            distance = (rows - cols) + tile * BLK
            inside = jnp.zeros((BLK, BLK), jnp.bool_)
            for band in range(NS):
                start = starts[band, first_head + head]
                width = widths[band, first_head + head]
                inside = inside | ((distance >= start) & (distance < start + width))
            bias[FIRST_BAND + head * REACH + tile] = jnp.where(inside, 0.0, OFF)


def make_index(blocks, picks, ctx, tp, index):
    first_own = PREFIX_BLOCKS + ctx * CHUNKS

    @pl.loop(0, HEADS)
    def per_head(head):
        picked = [picks[slot, tp * HEADS + head] == 1 for slot in range(NG)]
        listed = [blocks[tp, slot] for slot in range(NG)]

        @pl.loop(0, CHUNKS)
        def vertical(chunk):
            own = first_own + chunk
            for slot in range(NG):
                seen = jnp.where(listed[slot] < own, OPEN, jnp.where(listed[slot] == own, CAUSAL, SHUT))
                index[chunk, head, slot] = jnp.where(picked[slot], seen, SHUT)

        @pl.loop(0, WINDOW)
        def window(tile):
            block = first_own + tile - (REACH - 1)
            shut = block < PREFIX_BLOCKS
            for slot in range(NG):
                shut = shut | (picked[slot] & (listed[slot] == block))
            for chunk in range(CHUNKS):
                back = chunk + (REACH - 1) - tile
                outside = shut | (back < 0) | (back >= REACH)
                index[chunk, head, NG + tile] = jnp.where(outside, SHUT, FIRST_BAND + head * REACH + back)


def kernel(
    blocks, picks, starts, widths, q_hbm, prefix_hbm, fresh_hbm, w_hbm, out,
    kv_k, kv_v, win, q, w, w_in, mine, far_in, near_in, piece_in, vert, bias, index,
    m_s, l_s, acc_s, s_s, p_s, att, att_in, terms, kept, own_s, far_y, near_y,
    load_sem, send_sem, recv_sem,
):
    ctx = lax.axis_index("ctx")
    tp = lax.axis_index("tp")
    x, z = ctx // Z_SIZE, ctx % Z_SIZE
    y, core = tp // 2, tp % 2
    x_far, x_right, x_left = (x + 2) % X_SIZE, (x + 1) % X_SIZE, (x + 3) % X_SIZE
    y_far, y_right, y_left = (y + 2) % Y_SIZE, (y + 1) % Y_SIZE, (y + 3) % Y_SIZE
    turned = z == WRAP_COLUMN
    x_a = jnp.where(turned, x_left, x_right)
    x_b = jnp.where(turned, x_right, x_left)
    side_a = (x_a * Z_SIZE + z, tp)
    side_b = (x_b * Z_SIZE + z, tp)
    right = (x_right * Z_SIZE + z, tp)
    left = (x_left * Z_SIZE + z, tp)
    along = [(x * Z_SIZE + (z + k) % Z_SIZE, tp) for k in range(1, Z_SIZE)]
    size = X_SIZE * Z_SIZE
    after = ((ctx + 1) % size, tp)
    before = ((ctx + size - 1) % size, tp)
    pair = (ctx, y * 2 + (1 - core))
    up = (ctx, y_right * 2 + core)
    down = (ctx, y_left * 2 + core)
    barrier = pltpu.get_barrier_semaphore()
    partners = [right, left] + along + [after, before, pair, up, down]
    for device in partners:
        pl.semaphore_signal(barrier, inc=1, device_id=device, device_id_type=MESH)

    kv = (kv_k, kv_v)
    loads = []

    def load(src, dst):
        copy = pltpu.make_async_copy(src, dst, load_sem.at[len(loads)])
        copy.start()
        loads.append(copy)
        return copy

    kv_loads = [
        (
            load(prefix_hbm.at[part], kv[part].at[pl.ds(0, PREFIX_DEV)]),
            load(fresh_hbm.at[part], kv[part].at[pl.ds(PREFIX_DEV, FRESH_DEV)]),
        )
        for part in range(2)
    ]
    win_loads = [load(fresh_hbm.at[part], win.at[part, pl.ds(WINDOW - FRESH_DEV, FRESH_DEV)]) for part in range(2)]
    q_load = load(q_hbm, q)
    w_load = load(w_hbm, w)
    sends = Sends(send_sem, recv_sem)

    def rows(start, count):
        return pl.ds(pl.multiple_of(start, PIECE), count)

    def pick(part, quarter):
        for step in range(NG // X_SIZE):
            slot = quarter * (NG // X_SIZE) + step
            block = blocks[tp, slot]
            at_prefix = block - ctx * PREFIX_DEV
            at_fresh = block - PREFIX_BLOCKS - ctx * FRESH_DEV
            in_prefix = (at_prefix >= 0) & (at_prefix < PREFIX_DEV)
            in_fresh = (at_fresh >= 0) & (at_fresh < FRESH_DEV)
            row = jnp.where(in_prefix, at_prefix, jnp.where(in_fresh, PREFIX_DEV + at_fresh, 0))
            value = kv[part][row]
            mine[part, rows(slot * BLK, BLK), :] = jnp.where(in_prefix | in_fresh, value, jnp.zeros_like(value))

    def hand_on(part, age):
        src = WINDOW - FRESH_DEV * (1 + age)
        return sends.start(
            win.at[part, pl.ds(src, FRESH_DEV)], win.at[part, pl.ds(src - FRESH_DEV, FRESH_DEV)], after
        )

    far, near, window, pieces, gathered, spread, relayed = {}, {}, {}, {}, {}, {}, {}
    def far_start(part):
        far[part] = [
            sends.start(mine.at[part, rows(x_far * QUARTER, HALF), :], far_in.at[part, 0], side_a),
            sends.start(mine.at[part, rows(x_far * QUARTER + HALF, HALF), :], far_in.at[part, 1], left),
        ]

    def near_start(part):
        pick(part, x_right)
        pick(part, x_left)
        near[part] = [
            sends.start(mine.at[part, rows(x_b * QUARTER, HALF), :], near_in.at[part, 1, pl.ds(0, HALF), :], side_b),
            sends.start(
                mine.at[part, rows(x_right * QUARTER + HALF, HALF), :], near_in.at[part, 0, pl.ds(HALF, HALF), :], right
            ),
        ]

    def relay_x(part):
        far[part][0].wait_recv()
        mine[part, rows(x_a * QUARTER, HALF), :] += far_in[part, 0]
        near[part].append(
            sends.start(mine.at[part, rows(x_a * QUARTER, HALF), :], near_in.at[part, 0, pl.ds(0, HALF), :], side_a)
        )
        far[part][1].wait_recv()
        mine[part, rows(x_left * QUARTER + HALF, HALF), :] += far_in[part, 1]
        near[part].append(
            sends.start(
                mine.at[part, rows(x_left * QUARTER + HALF, HALF), :], near_in.at[part, 1, pl.ds(HALF, HALF), :], left
            )
        )

    def start_window():
        for part in range(2):
            win_loads[part].wait()
            window[part, 0] = hand_on(part, 0)

    def scatter_z(part):
        for copy in near[part]:
            copy.wait_recv()
        own = rows(x * QUARTER, QUARTER)
        mine[part, own, :] = mine[part, own, :] + near_in[part, 0] + near_in[part, 1]
        pieces[part] = [
            sends.start(
                mine.at[part, rows(x * QUARTER + (z + k) % Z_SIZE * PIECE, PIECE), :],
                piece_in.at[part, k - 1],
                along[k - 1],
            )
            for k in range(1, Z_SIZE)
        ]

    def gather_z(part):
        at = rows(x * QUARTER + z * PIECE, PIECE)
        total = mine[part, at, :]
        for k in range(1, Z_SIZE):
            pieces[part][k - 1].wait_recv()
            total = total + piece_in[part, k - 1]
        vert[part, at, :] = total
        gathered[part] = [
            sends.start(vert.at[part, at, :], vert.at[part, at, :], along[k - 1]) for k in range(1, Z_SIZE)
        ]

    def spread_x(part):
        for copy in gathered[part]:
            copy.wait_recv()
        top = rows(x * QUARTER, HALF)
        low = rows(x * QUARTER + HALF, HALF)
        spread[part] = [
            sends.start(vert.at[part, at, :], vert.at[part, at, :], device)
            for at, device in ((top, side_a), (low, left), (top, side_b), (low, right))
        ]

    def relay_back(part):
        spread[part][0].wait_recv()
        at = rows(x_b * QUARTER, HALF)
        relayed[part] = [sends.start(vert.at[part, at, :], vert.at[part, at, :], side_a)]
        spread[part][1].wait_recv()
        at = rows(x_right * QUARTER + HALF, HALF)
        relayed[part].append(sends.start(vert.at[part, at, :], vert.at[part, at, :], left))

    def complete(part):
        spread[part][2].wait_recv()
        spread[part][3].wait_recv()
        for copy in relayed[part]:
            copy.wait_recv()

    def pass_window(age):
        for part in range(2):
            window[part, age].wait_recv()
            if age < 2:
                window[part, age + 1] = hand_on(part, age + 1)

    def queries(chunk, head):
        return q[pl.ds(pl.multiple_of(chunk * BLK, BLK), BLK), head * HD : (head + 1) * HD]

    def head_rows(head):
        return slice(head * BLK, (head + 1) * BLK)

    def score(chunk, head, keys, tile, column, count, best):
        s = lax.dot_general(queries(chunk, head), keys, TRANSPOSED, preferred_element_type=F32)
        for j in range(count):
            piece = s[:, j * BLK : (j + 1) * BLK] + bias[index[chunk, head, tile + j]]
            s_s[head_rows(head), (column + j) * BLK : (column + j + 1) * BLK] = piece
            best = piece if best is None else jnp.maximum(best, piece)
        return best

    def weigh(head, top, column, count, total):
        probs = []
        for j in range(count):
            piece = s_s[head_rows(head), (column + j) * BLK : (column + j + 1) * BLK]
            piece = jnp.exp2((piece - top) * EXP_SCALE)
            total = piece if total is None else total + piece
            probs.append(piece.astype(BF16))
        return jnp.concatenate(probs, axis=1), total

    def wide(best):
        return jnp.broadcast_to(jnp.max(best, axis=1, keepdims=True), (BLK, BLK))

    def band(chunks, first, count, begin):
        @pl.loop(*chunks)
        def per_chunk(chunk):
            keys = win[0, first : first + count].reshape(count * BLK, HD)
            values = win[1, first : first + count].reshape(count * BLK, HD)
            best = None
            for head in range(HEADS + 1):
                fresh = None
                if head < HEADS:
                    fresh = score(chunk, head, keys, NG + first, 0, count, None)
                if head > 0:
                    done = head_rows(head - 1)
                    top = wide(best)
                    if not begin:
                        top = jnp.maximum(m_s[chunk, done, :], top)
                    probs, total = weigh(head - 1, top, 0, count, None)
                    product = jnp.dot(probs, values, preferred_element_type=F32)
                    if begin:
                        l_s[chunk, done, :] = total
                        acc_s[chunk, done, :] = product
                    else:
                        fade = jnp.exp2((m_s[chunk, done, :] - top) * EXP_SCALE)
                        l_s[chunk, done, :] = l_s[chunk, done, :] * fade + total
                        acc_s[chunk, done, :] = acc_s[chunk, done, :] * fade + product
                    m_s[chunk, done, :] = top
                best = fresh

    def vertical_scores(chunks):
        step = NG // 2

        @pl.loop(*chunks)
        def per_chunk(chunk):
            best = None
            for head in range(HEADS + 1):
                if head > 0:
                    done = head_rows(head - 1)
                    top = jnp.maximum(m_s[chunk, done, :], wide(best))
                    fade = jnp.exp2((m_s[chunk, done, :] - top) * EXP_SCALE)
                    total = l_s[chunk, done, :] * fade
                best = None
                for first in (0, step):
                    if head < HEADS:
                        keys = vert[0, first * BLK : (first + step) * BLK, :]
                        best = score(chunk, head, keys, first, first, step, best)
                    if head > 0:
                        probs, total = weigh(head - 1, top, first, step, total)
                        p_s[chunk, done, first * BLK : (first + step) * BLK] = probs
                if head > 0:
                    acc_s[chunk, done, :] = acc_s[chunk, done, :] * fade
                    l_s[chunk, done, :] = total

    def vertical_values(chunks):
        @pl.loop(*chunks)
        def per_chunk(chunk):
            product = jnp.dot(p_s[chunk], vert[1], preferred_element_type=F32)
            result = (acc_s[chunk] + product) / jnp.sum(l_s[chunk], axis=1, keepdims=True)
            for head in range(HEADS):
                att[pl.ds(pl.multiple_of(chunk * BLK, BLK), BLK), head * HD : (head + 1) * HD] = result[
                    head_rows(head), :
                ].astype(BF16)

    span = TOK // UNITS
    part_rows = span // 2

    def exchange(half):
        at = pl.ds(half * span, span)
        return sends.start(att.at[at, :], att_in.at[at, :], pair)

    def term(half, to):
        columns = pl.ds(pl.multiple_of((to * 2 + core) * TOK, TOK), TOK)
        at = slice(half * span, (half + 1) * span)
        total = jnp.dot(att[at, :], w[:, columns], preferred_element_type=F32)
        return total + jnp.dot(att_in[at, :], w_in[to], preferred_element_type=F32)

    def cut(half):
        start = half * span
        return pl.ds(start, part_rows), pl.ds(start + part_rows, part_rows)

    far_sum, near_sum = {}, {}

    def project(half):
        top, low = cut(half)
        total = term(half, y_far)
        terms[0, top, :] = total[:part_rows].astype(BF16)
        terms[0, low, :] = total[part_rows:].astype(BF16)
        far_sum[half] = [
            sends.start(terms.at[0, top, :], far_y.at[half, 0], up),
            sends.start(terms.at[0, low, :], far_y.at[half, 1], down),
        ]
        total = term(half, y_right)
        terms[1, low, :] = total[part_rows:].astype(BF16)
        kept[half, 0] = total[:part_rows]
        near_sum[half] = [sends.start(terms.at[1, low, :], near_y.at[0, low, :], up)]
        total = term(half, y_left)
        terms[2, top, :] = total[:part_rows].astype(BF16)
        kept[half, 1] = total[part_rows:]
        near_sum[half].append(sends.start(terms.at[2, top, :], near_y.at[1, top, :], down))

    def project_own(half):
        own_s[half] = term(half, y)

    def relay_y(half):
        top, low = cut(half)
        far_sum[half][0].wait_recv()
        terms[1, top, :] = (kept[half, 0] + far_y[half, 0].astype(F32)).astype(BF16)
        near_sum[half].append(sends.start(terms.at[1, top, :], near_y.at[0, top, :], up))
        far_sum[half][1].wait_recv()
        terms[2, low, :] = (kept[half, 1] + far_y[half, 1].astype(F32)).astype(BF16)
        near_sum[half].append(sends.start(terms.at[2, low, :], near_y.at[1, low, :], down))

    def total_up(half):
        for copy in near_sum[half]:
            copy.wait_recv()
        at = slice(half * span, (half + 1) * span)
        out[at, :] = (own_s[half] + near_y[0, at, :].astype(F32) + near_y[1, at, :].astype(F32)).astype(BF16)

    weights = []

    def start_weights():
        for to in range(Y_SIZE):
            columns = pl.ds(pl.multiple_of((to * 2 + 1 - core) * TOK, TOK), TOK)
            weights.append(sends.start(w_hbm.at[:, columns], w_in.at[to], pair))

    for copy in kv_loads[0]:
        copy.wait()
    pick(0, x_far)
    pl.semaphore_wait(barrier, len(partners))
    far_start(0)
    near_start(0)
    for copy in kv_loads[1]:
        copy.wait()
    pick(1, x_far)
    far_start(1)
    start_window()
    pick(0, x)
    relay_x(0)
    near_start(1)
    pick(1, x)
    relay_x(1)
    start_weights()
    make_bias(starts, widths, tp * HEADS, bias)
    scatter_z(0)
    make_index(blocks, picks, ctx, tp, index)
    q_load.wait()
    scatter_z(1)
    pass_window(0)
    band((0, 2), 8, 8, True)
    gather_z(0)
    band((2, 3), 8, 8, True)
    gather_z(1)
    pass_window(1)
    band((3, 4), 8, 8, True)
    band((0, 2), 4, 4, False)
    spread_x(0)
    band((2, 4), 4, 4, False)
    spread_x(1)
    relay_back(0)
    pass_window(2)
    relay_back(1)
    band((0, 4), 0, 4, False)
    complete(0)
    vertical_scores((0, 1))
    complete(1)
    swapped = {}

    def values(unit):
        vertical_values((unit, unit + 1))
        swapped[unit] = exchange(unit)

    values(0)
    vertical_scores((1, 2))
    values(1)
    w_load.wait()
    for copy in weights:
        copy.wait_recv()
    swapped[0].wait_recv()
    project(0)
    vertical_scores((2, 3))
    values(2)
    swapped[1].wait_recv()
    project(1)
    relay_y(0)
    vertical_scores((3, 4))
    values(3)
    swapped[2].wait_recv()
    project(2)
    relay_y(1)
    swapped[3].wait_recv()
    project(3)
    relay_y(2)
    project_own(0)
    relay_y(3)
    for unit in range(1, UNITS):
        project_own(unit)
    for unit in range(UNITS):
        total_up(unit)
    sends.finish()


def local(queries, prefix_kv, fresh_kv, group_blocks, head_pick, band_start, band_width, o_weight):
    vmem = pl.BlockSpec(memory_space=pltpu.VMEM)
    smem = pl.BlockSpec(memory_space=pltpu.SMEM)
    hbm = pl.BlockSpec(memory_space=pl.ANY)
    return pl.pallas_call(
        kernel,
        out_shape=jax.ShapeDtypeStruct((TOK, TOK), BF16),
        in_specs=[smem] * 4 + [hbm] * 4,
        out_specs=vmem,
        scratch_shapes=[
            pltpu.VMEM((PREFIX_DEV + FRESH_DEV, BLK, HD), BF16),
            pltpu.VMEM((PREFIX_DEV + FRESH_DEV, BLK, HD), BF16),
            pltpu.VMEM((2, WINDOW, BLK, HD), BF16),
            pltpu.VMEM((TOK, HEADS * HD), BF16),
            pltpu.VMEM((TOK, QH * HD), BF16),
            pltpu.VMEM((Y_SIZE, TOK, TOK), BF16),
            pltpu.VMEM((2, NG * BLK, HD), BF16),
            pltpu.VMEM((2, 2, HALF, HD), BF16),
            pltpu.VMEM((2, 2, QUARTER, HD), BF16),
            pltpu.VMEM((2, Z_SIZE - 1, PIECE, HD), BF16),
            pltpu.VMEM((2, NG * BLK, HD), BF16),
            pltpu.VMEM((BIAS_TILES, BLK, BLK), F32),
            pltpu.SMEM((CHUNKS, HEADS, NG + WINDOW), jnp.int32),
            pltpu.VMEM((CHUNKS, ROWS, BLK), F32),
            pltpu.VMEM((CHUNKS, ROWS, BLK), F32),
            pltpu.VMEM((CHUNKS, ROWS, HD), F32),
            pltpu.VMEM((ROWS, NG * BLK), F32),
            pltpu.VMEM((CHUNKS, ROWS, NG * BLK), BF16),
            pltpu.VMEM((TOK, HEADS * HD), BF16),
            pltpu.VMEM((TOK, HEADS * HD), BF16),
            pltpu.VMEM((3, TOK, TOK), BF16),
            pltpu.VMEM((UNITS, 2, TOK // UNITS // 2, TOK), F32),
            pltpu.VMEM((UNITS, TOK // UNITS, TOK), F32),
            pltpu.VMEM((UNITS, 2, TOK // UNITS // 2, TOK), BF16),
            pltpu.VMEM((2, TOK, TOK), BF16),
            pltpu.SemaphoreType.DMA((LOADS,)),
            pltpu.SemaphoreType.DMA((COPIES,)),
            pltpu.SemaphoreType.DMA((COPIES,)),
        ],
        compiler_params=pltpu.CompilerParams(
            vmem_limit_bytes=56 * 2**20, collective_id=0, has_side_effects=True
        ),
    )(
        group_blocks,
        head_pick.T,
        band_start.T,
        band_width.T,
        queries,
        prefix_kv.reshape(2, PREFIX_DEV, BLK, HD),
        fresh_kv.reshape(2, FRESH_DEV, BLK, HD),
        o_weight,
    )


def solution(mesh):
    return jax.shard_map(
        local,
        mesh=mesh,
        in_specs=(
            P("ctx", "tp"),
            P(None, "ctx", "tp"),
            P(None, "ctx", "tp"),
            P(),
            P(),
            P(),
            P(),
            P("tp", None),
        ),
        out_specs=P("ctx", "tp"),
        check_vma=False,
    )
```

```python
import math

import jax
import jax.numpy as jnp
from jax import lax
from jax.experimental import pallas as pl
from jax.experimental.pallas import tpu as pltpu
from jax.sharding import PartitionSpec as P

QH = 32
KVH = 8
HD = 128
BLK = 128
NG = 16
NS = 4
TOK = 512
PREFIX_BLOCKS = 512
CHUNKS = TOK // BLK
HEADS = QH // KVH
ROWS = HEADS * BLK
WINDOW = 16
REACH = 13
X_SIZE = 4
Z_SIZE = 8
Y_SIZE = 4
QUARTER = NG * BLK // X_SIZE
HALF = QUARTER // 2
PIECE = QUARTER // Z_SIZE
PREFIX_DEV = 16
FRESH_DEV = 4
COPIES = 96
UNITS = 4
WRAP_COLUMN = 0
LOADS = 14
OFF = -1e30
EXP_SCALE = math.log2(math.e) / math.sqrt(HD)
OPEN, SHUT, CAUSAL, FIRST_BAND = 0, 1, 2, 3
BIAS_TILES = FIRST_BAND + HEADS * REACH
MESH = pl.DeviceIdType.MESH
BF16 = jnp.bfloat16
F32 = jnp.float32
TRANSPOSED = (((1,), (1,)), ((), ()))


class Sends:
    def __init__(self, send_sem, recv_sem):
        self.send_sem, self.recv_sem, self.started = send_sem, recv_sem, []

    def start(self, src, dst, device):
        slot = len(self.started)
        copy = pltpu.make_async_remote_copy(
            src_ref=src,
            dst_ref=dst,
            send_sem=self.send_sem.at[slot],
            recv_sem=self.recv_sem.at[slot],
            device_id=device,
            device_id_type=MESH,
        )
        copy.start()
        self.started.append(copy)
        return copy

    def finish(self):
        for copy in self.started:
            copy.wait_send()


def make_bias(starts, widths, first_head, bias):
    rows = lax.broadcasted_iota(jnp.int32, (BLK, BLK), 0)
    cols = lax.broadcasted_iota(jnp.int32, (BLK, BLK), 1)
    bias[OPEN] = jnp.zeros((BLK, BLK), F32)
    bias[SHUT] = jnp.full((BLK, BLK), OFF, F32)
    bias[CAUSAL] = jnp.where(rows >= cols, 0.0, OFF)

    @pl.loop(0, HEADS)
    def per_head(head):
        @pl.loop(0, REACH)
        def per_tile(tile):
            distance = (rows - cols) + tile * BLK
            inside = jnp.zeros((BLK, BLK), jnp.bool_)
            for band in range(NS):
                start = starts[band, first_head + head]
                width = widths[band, first_head + head]
                inside = inside | ((distance >= start) & (distance < start + width))
            bias[FIRST_BAND + head * REACH + tile] = jnp.where(inside, 0.0, OFF)


def make_index(blocks, picks, ctx, tp, index):
    first_own = PREFIX_BLOCKS + ctx * CHUNKS

    @pl.loop(0, HEADS)
    def per_head(head):
        picked = [picks[slot, tp * HEADS + head] == 1 for slot in range(NG)]
        listed = [blocks[tp, slot] for slot in range(NG)]

        @pl.loop(0, CHUNKS)
        def vertical(chunk):
            own = first_own + chunk
            for slot in range(NG):
                seen = jnp.where(listed[slot] < own, OPEN, jnp.where(listed[slot] == own, CAUSAL, SHUT))
                index[chunk, head, slot] = jnp.where(picked[slot], seen, SHUT)

        @pl.loop(0, WINDOW)
        def window(tile):
            block = first_own + tile - (REACH - 1)
            shut = block < PREFIX_BLOCKS
            for slot in range(NG):
                shut = shut | (picked[slot] & (listed[slot] == block))
            for chunk in range(CHUNKS):
                back = chunk + (REACH - 1) - tile
                outside = shut | (back < 0) | (back >= REACH)
                index[chunk, head, NG + tile] = jnp.where(outside, SHUT, FIRST_BAND + head * REACH + back)


def kernel(
    blocks, picks, starts, widths, q_hbm, prefix_hbm, fresh_hbm, w_hbm, out,
    kv_k, kv_v, win, q, w, w_in, mine, far_in, near_in, piece_in, vert, bias, index,
    m_s, l_s, acc_s, s_s, p_s, att, att_in, terms, kept, own_s, far_y, near_y,
    load_sem, send_sem, recv_sem, reached,
):
    ctx = lax.axis_index("ctx")
    tp = lax.axis_index("tp")
    x, z = ctx // Z_SIZE, ctx % Z_SIZE
    y, core = tp // 2, tp % 2
    x_far, x_right, x_left = (x + 2) % X_SIZE, (x + 1) % X_SIZE, (x + 3) % X_SIZE
    y_far, y_right, y_left = (y + 2) % Y_SIZE, (y + 1) % Y_SIZE, (y + 3) % Y_SIZE
    turned = z == WRAP_COLUMN
    x_a = jnp.where(turned, x_left, x_right)
    x_b = jnp.where(turned, x_right, x_left)
    side_a = (x_a * Z_SIZE + z, tp)
    side_b = (x_b * Z_SIZE + z, tp)
    right = (x_right * Z_SIZE + z, tp)
    left = (x_left * Z_SIZE + z, tp)
    along = [(x * Z_SIZE + (z + k) % Z_SIZE, tp) for k in range(1, Z_SIZE)]
    size = X_SIZE * Z_SIZE
    after = ((ctx + 1) % size, tp)
    before = ((ctx + size - 1) % size, tp)
    pair = (ctx, y * 2 + (1 - core))
    up = (ctx, y_right * 2 + core)
    down = (ctx, y_left * 2 + core)
    barrier = pltpu.get_barrier_semaphore()
    two_on, two_back = along[1], along[Z_SIZE - 3]
    partners = [right, left, along[0], two_on, two_back, along[Z_SIZE - 2], after, before, pair, up, down]
    for device in partners:
        pl.semaphore_signal(barrier, inc=1, device_id=device, device_id_type=MESH)

    kv = (kv_k, kv_v)
    loads = []

    def load(src, dst):
        copy = pltpu.make_async_copy(src, dst, load_sem.at[len(loads)])
        copy.start()
        loads.append(copy)
        return copy

    kv_loads = [
        (
            load(prefix_hbm.at[part], kv[part].at[pl.ds(0, PREFIX_DEV)]),
            load(fresh_hbm.at[part], kv[part].at[pl.ds(PREFIX_DEV, FRESH_DEV)]),
        )
        for part in range(2)
    ]
    win_loads = [load(fresh_hbm.at[part], win.at[part, pl.ds(WINDOW - FRESH_DEV, FRESH_DEV)]) for part in range(2)]
    q_load = load(q_hbm, q)
    w_load = load(w_hbm, w)
    sends = Sends(send_sem, recv_sem)

    def rows(start, count):
        return pl.ds(pl.multiple_of(start, PIECE), count)

    def pick(part, quarter):
        for step in range(NG // X_SIZE):
            slot = quarter * (NG // X_SIZE) + step
            block = blocks[tp, slot]
            at_prefix = block - ctx * PREFIX_DEV
            at_fresh = block - PREFIX_BLOCKS - ctx * FRESH_DEV
            in_prefix = (at_prefix >= 0) & (at_prefix < PREFIX_DEV)
            in_fresh = (at_fresh >= 0) & (at_fresh < FRESH_DEV)
            row = jnp.where(in_prefix, at_prefix, jnp.where(in_fresh, PREFIX_DEV + at_fresh, 0))
            value = kv[part][row]
            mine[part, rows(slot * BLK, BLK), :] = jnp.where(in_prefix | in_fresh, value, jnp.zeros_like(value))

    def hand_on(part, age):
        src = WINDOW - FRESH_DEV * (1 + age)
        return sends.start(
            win.at[part, pl.ds(src, FRESH_DEV)], win.at[part, pl.ds(src - FRESH_DEV, FRESH_DEV)], after
        )

    far, near, window, pieces, gathered, spread, relayed = {}, {}, {}, {}, {}, {}, {}
    def far_start(part):
        far[part] = [
            sends.start(mine.at[part, rows(x_far * QUARTER, HALF), :], far_in.at[part, 0], side_a),
            sends.start(mine.at[part, rows(x_far * QUARTER + HALF, HALF), :], far_in.at[part, 1], left),
        ]

    def near_start(part):
        pick(part, x_right)
        pick(part, x_left)
        near[part] = [
            sends.start(mine.at[part, rows(x_b * QUARTER, HALF), :], near_in.at[part, 1, pl.ds(0, HALF), :], side_b),
            sends.start(
                mine.at[part, rows(x_right * QUARTER + HALF, HALF), :], near_in.at[part, 0, pl.ds(HALF, HALF), :], right
            ),
        ]

    def relay_x(part):
        far[part][0].wait_recv()
        mine[part, rows(x_a * QUARTER, HALF), :] += far_in[part, 0]
        near[part].append(
            sends.start(mine.at[part, rows(x_a * QUARTER, HALF), :], near_in.at[part, 0, pl.ds(0, HALF), :], side_a)
        )
        far[part][1].wait_recv()
        mine[part, rows(x_left * QUARTER + HALF, HALF), :] += far_in[part, 1]
        near[part].append(
            sends.start(
                mine.at[part, rows(x_left * QUARTER + HALF, HALF), :], near_in.at[part, 1, pl.ds(HALF, HALF), :], left
            )
        )

    def start_window():
        for part in range(2):
            win_loads[part].wait()
            window[part, 0] = hand_on(part, 0)

    def scatter_z(part):
        for copy in near[part]:
            copy.wait_recv()
        own = rows(x * QUARTER, QUARTER)
        mine[part, own, :] = mine[part, own, :] + near_in[part, 0] + near_in[part, 1]
        pieces[part] = [
            sends.start(
                mine.at[part, rows(x * QUARTER + (z + k) % Z_SIZE * PIECE, PIECE), :],
                piece_in.at[part, k - 1],
                along[k - 1],
            )
            for k in range(1, Z_SIZE)
        ]

    def gather_z(part):
        at = rows(x * QUARTER + z * PIECE, PIECE)
        total = mine[part, at, :]
        for k in range(1, Z_SIZE):
            pieces[part][k - 1].wait_recv()
            total = total + piece_in[part, k - 1]
        vert[part, at, :] = total
        gathered[part] = [
            sends.start(vert.at[part, at, :], vert.at[part, at, :], along[k - 1]) for k in range(1, Z_SIZE)
        ]

    def spread_x(part):
        for copy in gathered[part]:
            copy.wait_recv()
        top = rows(x * QUARTER, HALF)
        low = rows(x * QUARTER + HALF, HALF)
        spread[part] = [
            sends.start(vert.at[part, at, :], vert.at[part, at, :], device)
            for at, device in ((top, side_a), (low, left), (top, side_b), (low, right))
        ]

    def relay_back(part):
        spread[part][0].wait_recv()
        at = rows(x_b * QUARTER, HALF)
        relayed[part] = [sends.start(vert.at[part, at, :], vert.at[part, at, :], side_a)]
        spread[part][1].wait_recv()
        at = rows(x_right * QUARTER + HALF, HALF)
        relayed[part].append(sends.start(vert.at[part, at, :], vert.at[part, at, :], left))

    def complete(part):
        spread[part][2].wait_recv()
        spread[part][3].wait_recv()
        for copy in relayed[part]:
            copy.wait_recv()

    def pass_window(age):
        for part in range(2):
            window[part, age].wait_recv()
            if age < 2:
                window[part, age + 1] = hand_on(part, age + 1)

    def queries(chunk, head):
        return q[pl.ds(pl.multiple_of(chunk * BLK, BLK), BLK), head * HD : (head + 1) * HD]

    def head_rows(head):
        return slice(head * BLK, (head + 1) * BLK)

    def score(chunk, head, keys, tile, column, count, best):
        s = lax.dot_general(queries(chunk, head), keys, TRANSPOSED, preferred_element_type=F32)
        for j in range(count):
            piece = s[:, j * BLK : (j + 1) * BLK] + bias[index[chunk, head, tile + j]]
            s_s[head_rows(head), (column + j) * BLK : (column + j + 1) * BLK] = piece
            best = piece if best is None else jnp.maximum(best, piece)
        return best

    def weigh(head, top, column, count, total):
        probs = []
        for j in range(count):
            piece = s_s[head_rows(head), (column + j) * BLK : (column + j + 1) * BLK]
            piece = jnp.exp2((piece - top) * EXP_SCALE)
            total = piece if total is None else total + piece
            probs.append(piece.astype(BF16))
        return jnp.concatenate(probs, axis=1), total

    def wide(best):
        return jnp.broadcast_to(jnp.max(best, axis=1, keepdims=True), (BLK, BLK))

    def band(chunks, first, count, begin):
        @pl.loop(*chunks)
        def per_chunk(chunk):
            keys = win[0, first : first + count].reshape(count * BLK, HD)
            values = win[1, first : first + count].reshape(count * BLK, HD)
            best = None
            for head in range(HEADS + 1):
                fresh = None
                if head < HEADS:
                    fresh = score(chunk, head, keys, NG + first, 0, count, None)
                if head > 0:
                    done = head_rows(head - 1)
                    top = wide(best)
                    if not begin:
                        top = jnp.maximum(m_s[chunk, done, :], top)
                    probs, total = weigh(head - 1, top, 0, count, None)
                    product = jnp.dot(probs, values, preferred_element_type=F32)
                    if begin:
                        l_s[chunk, done, :] = total
                        acc_s[chunk, done, :] = product
                    else:
                        fade = jnp.exp2((m_s[chunk, done, :] - top) * EXP_SCALE)
                        l_s[chunk, done, :] = l_s[chunk, done, :] * fade + total
                        acc_s[chunk, done, :] = acc_s[chunk, done, :] * fade + product
                    m_s[chunk, done, :] = top
                best = fresh

    def vertical_scores(chunks):
        step = NG // 2

        @pl.loop(*chunks)
        def per_chunk(chunk):
            best = None
            for head in range(HEADS + 1):
                if head > 0:
                    done = head_rows(head - 1)
                    top = jnp.maximum(m_s[chunk, done, :], wide(best))
                    fade = jnp.exp2((m_s[chunk, done, :] - top) * EXP_SCALE)
                    total = l_s[chunk, done, :] * fade
                best = None
                for first in (0, step):
                    if head < HEADS:
                        keys = vert[0, first * BLK : (first + step) * BLK, :]
                        best = score(chunk, head, keys, first, first, step, best)
                    if head > 0:
                        probs, total = weigh(head - 1, top, first, step, total)
                        p_s[chunk, done, first * BLK : (first + step) * BLK] = probs
                if head > 0:
                    acc_s[chunk, done, :] = acc_s[chunk, done, :] * fade
                    l_s[chunk, done, :] = total

    def vertical_values(chunks):
        @pl.loop(*chunks)
        def per_chunk(chunk):
            product = jnp.dot(p_s[chunk], vert[1], preferred_element_type=F32)
            result = (acc_s[chunk] + product) / jnp.sum(l_s[chunk], axis=1, keepdims=True)
            for head in range(HEADS):
                att[pl.ds(pl.multiple_of(chunk * BLK, BLK), BLK), head * HD : (head + 1) * HD] = result[
                    head_rows(head), :
                ].astype(BF16)

    span = TOK // UNITS
    part_rows = span // 2

    def exchange(half):
        at = pl.ds(half * span, span)
        return sends.start(att.at[at, :], att_in.at[at, :], pair)

    def term(half, to):
        columns = pl.ds(pl.multiple_of((to * 2 + core) * TOK, TOK), TOK)
        at = slice(half * span, (half + 1) * span)
        total = jnp.dot(att[at, :], w[:, columns], preferred_element_type=F32)
        return total + jnp.dot(att_in[at, :], w_in[to], preferred_element_type=F32)

    def cut(half):
        start = half * span
        return pl.ds(start, part_rows), pl.ds(start + part_rows, part_rows)

    far_sum, near_sum = {}, {}

    def project(half):
        top, low = cut(half)
        total = term(half, y_far)
        terms[0, top, :] = total[:part_rows].astype(BF16)
        terms[0, low, :] = total[part_rows:].astype(BF16)
        far_sum[half] = [
            sends.start(terms.at[0, top, :], far_y.at[half, 0], up),
            sends.start(terms.at[0, low, :], far_y.at[half, 1], down),
        ]
        total = term(half, y_right)
        terms[1, low, :] = total[part_rows:].astype(BF16)
        kept[half, 0] = total[:part_rows]
        near_sum[half] = [sends.start(terms.at[1, low, :], near_y.at[0, low, :], up)]
        total = term(half, y_left)
        terms[2, top, :] = total[:part_rows].astype(BF16)
        kept[half, 1] = total[part_rows:]
        near_sum[half].append(sends.start(terms.at[2, top, :], near_y.at[1, top, :], down))

    def project_own(half):
        own_s[half] = term(half, y)

    def relay_y(half):
        top, low = cut(half)
        far_sum[half][0].wait_recv()
        terms[1, top, :] = (kept[half, 0] + far_y[half, 0].astype(F32)).astype(BF16)
        near_sum[half].append(sends.start(terms.at[1, top, :], near_y.at[0, top, :], up))
        far_sum[half][1].wait_recv()
        terms[2, low, :] = (kept[half, 1] + far_y[half, 1].astype(F32)).astype(BF16)
        near_sum[half].append(sends.start(terms.at[2, low, :], near_y.at[1, low, :], down))

    def total_up(half):
        for copy in near_sum[half]:
            copy.wait_recv()
        at = slice(half * span, (half + 1) * span)
        out[at, :] = (own_s[half] + near_y[0, at, :].astype(F32) + near_y[1, at, :].astype(F32)).astype(BF16)

    weights = []

    def start_weights():
        for to in range(Y_SIZE):
            columns = pl.ds(pl.multiple_of((to * 2 + 1 - core) * TOK, TOK), TOK)
            weights.append(sends.start(w_hbm.at[:, columns], w_in.at[to], pair))

    for copy in kv_loads[0]:
        copy.wait()
    pick(0, x_far)
    pl.semaphore_wait(barrier, len(partners))
    for device in (two_on, two_back):
        pl.semaphore_signal(reached, inc=1, device_id=device, device_id_type=MESH)
    far_start(0)
    near_start(0)
    for copy in kv_loads[1]:
        copy.wait()
    pick(1, x_far)
    far_start(1)
    start_window()
    pick(0, x)
    relay_x(0)
    near_start(1)
    pick(1, x)
    relay_x(1)
    start_weights()
    make_bias(starts, widths, tp * HEADS, bias)
    pl.semaphore_wait(reached, 2)
    scatter_z(0)
    q_load.wait()
    scatter_z(1)
    make_index(blocks, picks, ctx, tp, index)
    pass_window(0)
    band((0, 2), 8, 8, True)
    gather_z(0)
    band((2, 3), 8, 8, True)
    gather_z(1)
    pass_window(1)
    band((3, 4), 8, 8, True)
    band((0, 2), 4, 4, False)
    spread_x(0)
    band((2, 4), 4, 4, False)
    spread_x(1)
    relay_back(0)
    pass_window(2)
    relay_back(1)
    band((0, 4), 0, 4, False)
    complete(0)
    vertical_scores((0, 1))
    complete(1)
    swapped = {}

    def values(unit):
        vertical_values((unit, unit + 1))
        swapped[unit] = exchange(unit)

    values(0)
    vertical_scores((1, 2))
    values(1)
    w_load.wait()
    for copy in weights:
        copy.wait_recv()
    swapped[0].wait_recv()
    project(0)
    vertical_scores((2, 3))
    values(2)
    swapped[1].wait_recv()
    project(1)
    relay_y(0)
    vertical_scores((3, 4))
    values(3)
    swapped[2].wait_recv()
    project(2)
    relay_y(1)
    swapped[3].wait_recv()
    project(3)
    relay_y(2)
    project_own(0)
    relay_y(3)
    for unit in range(1, UNITS):
        project_own(unit)
    for unit in range(UNITS):
        total_up(unit)
    sends.finish()


def local(queries, prefix_kv, fresh_kv, group_blocks, head_pick, band_start, band_width, o_weight):
    vmem = pl.BlockSpec(memory_space=pltpu.VMEM)
    smem = pl.BlockSpec(memory_space=pltpu.SMEM)
    hbm = pl.BlockSpec(memory_space=pl.ANY)
    return pl.pallas_call(
        kernel,
        out_shape=jax.ShapeDtypeStruct((TOK, TOK), BF16),
        in_specs=[smem] * 4 + [hbm] * 4,
        out_specs=vmem,
        scratch_shapes=[
            pltpu.VMEM((PREFIX_DEV + FRESH_DEV, BLK, HD), BF16),
            pltpu.VMEM((PREFIX_DEV + FRESH_DEV, BLK, HD), BF16),
            pltpu.VMEM((2, WINDOW, BLK, HD), BF16),
            pltpu.VMEM((TOK, HEADS * HD), BF16),
            pltpu.VMEM((TOK, QH * HD), BF16),
            pltpu.VMEM((Y_SIZE, TOK, TOK), BF16),
            pltpu.VMEM((2, NG * BLK, HD), BF16),
            pltpu.VMEM((2, 2, HALF, HD), BF16),
            pltpu.VMEM((2, 2, QUARTER, HD), BF16),
            pltpu.VMEM((2, Z_SIZE - 1, PIECE, HD), BF16),
            pltpu.VMEM((2, NG * BLK, HD), BF16),
            pltpu.VMEM((BIAS_TILES, BLK, BLK), F32),
            pltpu.SMEM((CHUNKS, HEADS, NG + WINDOW), jnp.int32),
            pltpu.VMEM((CHUNKS, ROWS, BLK), F32),
            pltpu.VMEM((CHUNKS, ROWS, BLK), F32),
            pltpu.VMEM((CHUNKS, ROWS, HD), F32),
            pltpu.VMEM((ROWS, NG * BLK), F32),
            pltpu.VMEM((CHUNKS, ROWS, NG * BLK), BF16),
            pltpu.VMEM((TOK, HEADS * HD), BF16),
            pltpu.VMEM((TOK, HEADS * HD), BF16),
            pltpu.VMEM((3, TOK, TOK), BF16),
            pltpu.VMEM((UNITS, 2, TOK // UNITS // 2, TOK), F32),
            pltpu.VMEM((UNITS, TOK // UNITS, TOK), F32),
            pltpu.VMEM((UNITS, 2, TOK // UNITS // 2, TOK), BF16),
            pltpu.VMEM((2, TOK, TOK), BF16),
            pltpu.SemaphoreType.DMA((LOADS,)),
            pltpu.SemaphoreType.DMA((COPIES,)),
            pltpu.SemaphoreType.DMA((COPIES,)),
            pltpu.SemaphoreType.REGULAR,
        ],
        compiler_params=pltpu.CompilerParams(
            vmem_limit_bytes=56 * 2**20, collective_id=0, has_side_effects=True
        ),
    )(
        group_blocks,
        head_pick.T,
        band_start.T,
        band_width.T,
        queries,
        prefix_kv.reshape(2, PREFIX_DEV, BLK, HD),
        fresh_kv.reshape(2, FRESH_DEV, BLK, HD),
        o_weight,
    )


def solution(mesh):
    return jax.shard_map(
        local,
        mesh=mesh,
        in_specs=(
            P("ctx", "tp"),
            P(None, "ctx", "tp"),
            P(None, "ctx", "tp"),
            P(),
            P(),
            P(),
            P(),
            P("tp", None),
        ),
        out_specs=P("ctx", "tp"),
        check_vma=False,
    )
```

```python
import math

import jax
import jax.numpy as jnp
from jax import lax
from jax.experimental import pallas as pl
from jax.experimental.pallas import tpu as pltpu
from jax.sharding import PartitionSpec as P

QH = 32
KVH = 8
HD = 128
BLK = 128
NG = 16
NS = 4
TOK = 512
PREFIX_BLOCKS = 512
CHUNKS = TOK // BLK
HEADS = QH // KVH
ROWS = HEADS * BLK
WINDOW = 16
REACH = 13
X_SIZE = 4
Z_SIZE = 8
Y_SIZE = 4
QUARTER = NG * BLK // X_SIZE
HALF = QUARTER // 2
PIECE = QUARTER // Z_SIZE
PREFIX_DEV = 16
FRESH_DEV = 4
COPIES = 96
UNITS = 4
WRAP_COLUMN = 0
LOADS = 14
OFF = -1e30
EXP_SCALE = math.log2(math.e) / math.sqrt(HD)
OPEN, SHUT, CAUSAL, FIRST_BAND = 0, 1, 2, 3
BIAS_TILES = FIRST_BAND + HEADS * REACH
MESH = pl.DeviceIdType.MESH
BF16 = jnp.bfloat16
F32 = jnp.float32
TRANSPOSED = (((1,), (1,)), ((), ()))


class Sends:
    def __init__(self, send_sem, recv_sem):
        self.send_sem, self.recv_sem, self.started = send_sem, recv_sem, []

    def start(self, src, dst, device):
        slot = len(self.started)
        copy = pltpu.make_async_remote_copy(
            src_ref=src,
            dst_ref=dst,
            send_sem=self.send_sem.at[slot],
            recv_sem=self.recv_sem.at[slot],
            device_id=device,
            device_id_type=MESH,
        )
        copy.start()
        self.started.append(copy)
        return copy

    def finish(self):
        for copy in self.started:
            copy.wait_send()


def make_bias(starts, widths, first_head, bias):
    rows = lax.broadcasted_iota(jnp.int32, (BLK, BLK), 0)
    cols = lax.broadcasted_iota(jnp.int32, (BLK, BLK), 1)
    bias[OPEN] = jnp.zeros((BLK, BLK), F32)
    bias[SHUT] = jnp.full((BLK, BLK), OFF, F32)
    bias[CAUSAL] = jnp.where(rows >= cols, 0.0, OFF)

    @pl.loop(0, HEADS)
    def per_head(head):
        @pl.loop(0, REACH)
        def per_tile(tile):
            distance = (rows - cols) + tile * BLK
            inside = jnp.zeros((BLK, BLK), jnp.bool_)
            for band in range(NS):
                start = starts[band, first_head + head]
                width = widths[band, first_head + head]
                inside = inside | ((distance >= start) & (distance < start + width))
            bias[FIRST_BAND + head * REACH + tile] = jnp.where(inside, 0.0, OFF)


def make_index(blocks, picks, ctx, tp, index):
    first_own = PREFIX_BLOCKS + ctx * CHUNKS

    @pl.loop(0, HEADS)
    def per_head(head):
        picked = [picks[slot, tp * HEADS + head] == 1 for slot in range(NG)]
        listed = [blocks[tp, slot] for slot in range(NG)]

        @pl.loop(0, CHUNKS)
        def vertical(chunk):
            own = first_own + chunk
            for slot in range(NG):
                seen = jnp.where(listed[slot] < own, OPEN, jnp.where(listed[slot] == own, CAUSAL, SHUT))
                index[chunk, head, slot] = jnp.where(picked[slot], seen, SHUT)

        @pl.loop(0, WINDOW)
        def window(tile):
            block = first_own + tile - (REACH - 1)
            shut = block < PREFIX_BLOCKS
            for slot in range(NG):
                shut = shut | (picked[slot] & (listed[slot] == block))
            for chunk in range(CHUNKS):
                back = chunk + (REACH - 1) - tile
                outside = shut | (back < 0) | (back >= REACH)
                index[chunk, head, NG + tile] = jnp.where(outside, SHUT, FIRST_BAND + head * REACH + back)


def kernel(
    blocks, picks, starts, widths, q_hbm, prefix_hbm, fresh_hbm, w_hbm, out,
    kv_k, kv_v, win, q, w, w_in, mine, far_in, near_in, piece_in, vert, bias, index,
    m_s, l_s, acc_s, s_s, p_s, att, att_in, terms, kept, own_s, far_y, near_y,
    load_sem, send_sem, recv_sem, reached,
):
    ctx = lax.axis_index("ctx")
    tp = lax.axis_index("tp")
    x, z = ctx // Z_SIZE, ctx % Z_SIZE
    y, core = tp // 2, tp % 2
    x_far, x_right, x_left = (x + 2) % X_SIZE, (x + 1) % X_SIZE, (x + 3) % X_SIZE
    y_far, y_right, y_left = (y + 2) % Y_SIZE, (y + 1) % Y_SIZE, (y + 3) % Y_SIZE
    turned = z == WRAP_COLUMN
    x_a = jnp.where(turned, x_left, x_right)
    x_b = jnp.where(turned, x_right, x_left)
    side_a = (x_a * Z_SIZE + z, tp)
    side_b = (x_b * Z_SIZE + z, tp)
    x_back = x_left
    back_a = (x_right * Z_SIZE + z, tp)
    back_b = (x_left * Z_SIZE + z, tp)
    right = (x_right * Z_SIZE + z, tp)
    left = (x_left * Z_SIZE + z, tp)
    along = [(x * Z_SIZE + (z + k) % Z_SIZE, tp) for k in range(1, Z_SIZE)]
    size = X_SIZE * Z_SIZE
    after = ((ctx + 1) % size, tp)
    before = ((ctx + size - 1) % size, tp)
    pair = (ctx, y * 2 + (1 - core))
    up = (ctx, y_right * 2 + core)
    down = (ctx, y_left * 2 + core)
    barrier = pltpu.get_barrier_semaphore()
    two_on, two_back = along[1], along[Z_SIZE - 3]
    partners = [right, left, along[0], two_on, two_back, along[Z_SIZE - 2], after, before, pair, up, down]
    for device in partners:
        pl.semaphore_signal(barrier, inc=1, device_id=device, device_id_type=MESH)

    kv = (kv_k, kv_v)
    loads = []

    def load(src, dst):
        copy = pltpu.make_async_copy(src, dst, load_sem.at[len(loads)])
        copy.start()
        loads.append(copy)
        return copy

    kv_loads = [
        (
            load(prefix_hbm.at[part], kv[part].at[pl.ds(0, PREFIX_DEV)]),
            load(fresh_hbm.at[part], kv[part].at[pl.ds(PREFIX_DEV, FRESH_DEV)]),
        )
        for part in range(2)
    ]
    win_loads = [load(fresh_hbm.at[part], win.at[part, pl.ds(WINDOW - FRESH_DEV, FRESH_DEV)]) for part in range(2)]
    q_load = load(q_hbm, q)
    w_load = load(w_hbm, w)
    sends = Sends(send_sem, recv_sem)

    def rows(start, count):
        return pl.ds(pl.multiple_of(start, PIECE), count)

    def pick(part, quarter):
        for step in range(NG // X_SIZE):
            slot = quarter * (NG // X_SIZE) + step
            block = blocks[tp, slot]
            at_prefix = block - ctx * PREFIX_DEV
            at_fresh = block - PREFIX_BLOCKS - ctx * FRESH_DEV
            in_prefix = (at_prefix >= 0) & (at_prefix < PREFIX_DEV)
            in_fresh = (at_fresh >= 0) & (at_fresh < FRESH_DEV)
            row = jnp.where(in_prefix, at_prefix, jnp.where(in_fresh, PREFIX_DEV + at_fresh, 0))
            value = kv[part][row]
            mine[part, rows(slot * BLK, BLK), :] = jnp.where(in_prefix | in_fresh, value, jnp.zeros_like(value))

    def hand_on(part, age):
        src = WINDOW - FRESH_DEV * (1 + age)
        return sends.start(
            win.at[part, pl.ds(src, FRESH_DEV)], win.at[part, pl.ds(src - FRESH_DEV, FRESH_DEV)], after
        )

    far, near, window, pieces, gathered, spread, relayed = {}, {}, {}, {}, {}, {}, {}
    def far_start(part):
        far[part] = [
            sends.start(mine.at[part, rows(x_far * QUARTER, HALF), :], far_in.at[part, 0], side_a),
            sends.start(mine.at[part, rows(x_far * QUARTER + HALF, HALF), :], far_in.at[part, 1], left),
        ]

    def near_start(part):
        pick(part, x_right)
        pick(part, x_left)
        near[part] = [
            sends.start(mine.at[part, rows(x_b * QUARTER, HALF), :], near_in.at[part, 1, pl.ds(0, HALF), :], side_b),
            sends.start(
                mine.at[part, rows(x_right * QUARTER + HALF, HALF), :], near_in.at[part, 0, pl.ds(HALF, HALF), :], right
            ),
        ]

    def relay_x(part):
        far[part][0].wait_recv()
        mine[part, rows(x_a * QUARTER, HALF), :] += far_in[part, 0]
        near[part].append(
            sends.start(mine.at[part, rows(x_a * QUARTER, HALF), :], near_in.at[part, 0, pl.ds(0, HALF), :], side_a)
        )
        far[part][1].wait_recv()
        mine[part, rows(x_left * QUARTER + HALF, HALF), :] += far_in[part, 1]
        near[part].append(
            sends.start(
                mine.at[part, rows(x_left * QUARTER + HALF, HALF), :], near_in.at[part, 1, pl.ds(HALF, HALF), :], left
            )
        )

    def start_window():
        for part in range(2):
            win_loads[part].wait()
            window[part, 0] = hand_on(part, 0)

    def scatter_z(part):
        for copy in near[part]:
            copy.wait_recv()
        own = rows(x * QUARTER, QUARTER)
        mine[part, own, :] = mine[part, own, :] + near_in[part, 0] + near_in[part, 1]
        pieces[part] = [
            sends.start(
                mine.at[part, rows(x * QUARTER + (z + k) % Z_SIZE * PIECE, PIECE), :],
                piece_in.at[part, k - 1],
                along[k - 1],
            )
            for k in range(1, Z_SIZE)
        ]

    def gather_z(part):
        at = rows(x * QUARTER + z * PIECE, PIECE)
        total = mine[part, at, :]
        for k in range(1, Z_SIZE):
            pieces[part][k - 1].wait_recv()
            total = total + piece_in[part, k - 1]
        vert[part, at, :] = total
        gathered[part] = [
            sends.start(vert.at[part, at, :], vert.at[part, at, :], along[k - 1]) for k in range(1, Z_SIZE)
        ]

    def spread_x(part):
        for copy in gathered[part]:
            copy.wait_recv()
        top = rows(x * QUARTER, HALF)
        low = rows(x * QUARTER + HALF, HALF)
        spread[part] = [
            sends.start(vert.at[part, at, :], vert.at[part, at, :], device)
            for at, device in ((top, back_a), (low, left), (top, back_b), (low, right))
        ]

    def relay_back(part):
        spread[part][0].wait_recv()
        at = rows(x_back * QUARTER, HALF)
        relayed[part] = [sends.start(vert.at[part, at, :], vert.at[part, at, :], back_a)]
        spread[part][1].wait_recv()
        at = rows(x_right * QUARTER + HALF, HALF)
        relayed[part].append(sends.start(vert.at[part, at, :], vert.at[part, at, :], left))

    def complete(part):
        spread[part][2].wait_recv()
        spread[part][3].wait_recv()
        for copy in relayed[part]:
            copy.wait_recv()

    def pass_window(age):
        for part in range(2):
            window[part, age].wait_recv()
            if age < 2:
                window[part, age + 1] = hand_on(part, age + 1)

    def queries(chunk, head):
        return q[pl.ds(pl.multiple_of(chunk * BLK, BLK), BLK), head * HD : (head + 1) * HD]

    def head_rows(head):
        return slice(head * BLK, (head + 1) * BLK)

    def score(chunk, head, keys, tile, column, count, best):
        s = lax.dot_general(queries(chunk, head), keys, TRANSPOSED, preferred_element_type=F32)
        for j in range(count):
            piece = s[:, j * BLK : (j + 1) * BLK] + bias[index[chunk, head, tile + j]]
            s_s[head_rows(head), (column + j) * BLK : (column + j + 1) * BLK] = piece
            best = piece if best is None else jnp.maximum(best, piece)
        return best

    def weigh(head, top, column, count, total):
        probs = []
        for j in range(count):
            piece = s_s[head_rows(head), (column + j) * BLK : (column + j + 1) * BLK]
            piece = jnp.exp2((piece - top) * EXP_SCALE)
            total = piece if total is None else total + piece
            probs.append(piece.astype(BF16))
        return jnp.concatenate(probs, axis=1), total

    def wide(best):
        return jnp.broadcast_to(jnp.max(best, axis=1, keepdims=True), (BLK, BLK))

    def band(chunks, first, count, begin):
        @pl.loop(*chunks)
        def per_chunk(chunk):
            keys = win[0, first : first + count].reshape(count * BLK, HD)
            values = win[1, first : first + count].reshape(count * BLK, HD)
            best = None
            for head in range(HEADS + 1):
                fresh = None
                if head < HEADS:
                    fresh = score(chunk, head, keys, NG + first, 0, count, None)
                if head > 0:
                    done = head_rows(head - 1)
                    top = wide(best)
                    if not begin:
                        top = jnp.maximum(m_s[chunk, done, :], top)
                    probs, total = weigh(head - 1, top, 0, count, None)
                    product = jnp.dot(probs, values, preferred_element_type=F32)
                    if begin:
                        l_s[chunk, done, :] = total
                        acc_s[chunk, done, :] = product
                    else:
                        fade = jnp.exp2((m_s[chunk, done, :] - top) * EXP_SCALE)
                        l_s[chunk, done, :] = l_s[chunk, done, :] * fade + total
                        acc_s[chunk, done, :] = acc_s[chunk, done, :] * fade + product
                    m_s[chunk, done, :] = top
                best = fresh

    def vertical_scores(chunks):
        step = NG // 2

        @pl.loop(*chunks)
        def per_chunk(chunk):
            best = None
            for head in range(HEADS + 1):
                if head > 0:
                    done = head_rows(head - 1)
                    top = jnp.maximum(m_s[chunk, done, :], wide(best))
                    fade = jnp.exp2((m_s[chunk, done, :] - top) * EXP_SCALE)
                    total = l_s[chunk, done, :] * fade
                best = None
                for first in (0, step):
                    if head < HEADS:
                        keys = vert[0, first * BLK : (first + step) * BLK, :]
                        best = score(chunk, head, keys, first, first, step, best)
                    if head > 0:
                        probs, total = weigh(head - 1, top, first, step, total)
                        p_s[chunk, done, first * BLK : (first + step) * BLK] = probs
                if head > 0:
                    acc_s[chunk, done, :] = acc_s[chunk, done, :] * fade
                    l_s[chunk, done, :] = total

    def vertical_values(chunks):
        @pl.loop(*chunks)
        def per_chunk(chunk):
            product = jnp.dot(p_s[chunk], vert[1], preferred_element_type=F32)
            result = (acc_s[chunk] + product) / jnp.sum(l_s[chunk], axis=1, keepdims=True)
            for head in range(HEADS):
                att[pl.ds(pl.multiple_of(chunk * BLK, BLK), BLK), head * HD : (head + 1) * HD] = result[
                    head_rows(head), :
                ].astype(BF16)

    span = TOK // UNITS
    part_rows = span // 2

    def exchange(half):
        at = pl.ds(half * span, span)
        return sends.start(att.at[at, :], att_in.at[at, :], pair)

    def term(half, to):
        columns = pl.ds(pl.multiple_of((to * 2 + core) * TOK, TOK), TOK)
        at = slice(half * span, (half + 1) * span)
        total = jnp.dot(att[at, :], w[:, columns], preferred_element_type=F32)
        return total + jnp.dot(att_in[at, :], w_in[to], preferred_element_type=F32)

    def cut(half):
        start = half * span
        return pl.ds(start, part_rows), pl.ds(start + part_rows, part_rows)

    far_sum, near_sum = {}, {}

    def project(half):
        top, low = cut(half)
        total = term(half, y_far)
        terms[0, top, :] = total[:part_rows].astype(BF16)
        terms[0, low, :] = total[part_rows:].astype(BF16)
        far_sum[half] = [
            sends.start(terms.at[0, top, :], far_y.at[half, 0], up),
            sends.start(terms.at[0, low, :], far_y.at[half, 1], down),
        ]
        total = term(half, y_right)
        terms[1, low, :] = total[part_rows:].astype(BF16)
        kept[half, 0] = total[:part_rows]
        near_sum[half] = [sends.start(terms.at[1, low, :], near_y.at[0, low, :], up)]
        total = term(half, y_left)
        terms[2, top, :] = total[:part_rows].astype(BF16)
        kept[half, 1] = total[part_rows:]
        near_sum[half].append(sends.start(terms.at[2, top, :], near_y.at[1, top, :], down))

    def project_own(half):
        own_s[half] = term(half, y)

    def relay_y(half):
        top, low = cut(half)
        far_sum[half][0].wait_recv()
        terms[1, top, :] = (kept[half, 0] + far_y[half, 0].astype(F32)).astype(BF16)
        near_sum[half].append(sends.start(terms.at[1, top, :], near_y.at[0, top, :], up))
        far_sum[half][1].wait_recv()
        terms[2, low, :] = (kept[half, 1] + far_y[half, 1].astype(F32)).astype(BF16)
        near_sum[half].append(sends.start(terms.at[2, low, :], near_y.at[1, low, :], down))

    def total_up(half):
        for copy in near_sum[half]:
            copy.wait_recv()
        at = slice(half * span, (half + 1) * span)
        out[at, :] = (own_s[half] + near_y[0, at, :].astype(F32) + near_y[1, at, :].astype(F32)).astype(BF16)

    weights = []

    def start_weights():
        for to in range(Y_SIZE):
            columns = pl.ds(pl.multiple_of((to * 2 + 1 - core) * TOK, TOK), TOK)
            weights.append(sends.start(w_hbm.at[:, columns], w_in.at[to], pair))

    for copy in kv_loads[0]:
        copy.wait()
    pick(0, x_far)
    pl.semaphore_wait(barrier, len(partners))
    for device in (two_on, two_back):
        pl.semaphore_signal(reached, inc=1, device_id=device, device_id_type=MESH)
    far_start(0)
    near_start(0)
    for copy in kv_loads[1]:
        copy.wait()
    pick(1, x_far)
    far_start(1)
    start_window()
    pick(0, x)
    relay_x(0)
    near_start(1)
    pick(1, x)
    relay_x(1)
    start_weights()
    make_bias(starts, widths, tp * HEADS, bias)
    pl.semaphore_wait(reached, 2)
    scatter_z(0)
    q_load.wait()
    scatter_z(1)
    make_index(blocks, picks, ctx, tp, index)
    pass_window(0)
    band((0, 2), 8, 8, True)
    gather_z(0)
    band((2, 3), 8, 8, True)
    gather_z(1)
    pass_window(1)
    band((3, 4), 8, 8, True)
    band((0, 2), 4, 4, False)
    spread_x(0)
    band((2, 4), 4, 4, False)
    spread_x(1)
    relay_back(0)
    pass_window(2)
    relay_back(1)
    band((0, 4), 0, 4, False)
    complete(0)
    vertical_scores((0, 1))
    complete(1)
    swapped = {}

    def values(unit):
        vertical_values((unit, unit + 1))
        swapped[unit] = exchange(unit)

    values(0)
    vertical_scores((1, 2))
    values(1)
    w_load.wait()
    for copy in weights:
        copy.wait_recv()
    swapped[0].wait_recv()
    project(0)
    vertical_scores((2, 3))
    values(2)
    swapped[1].wait_recv()
    project(1)
    relay_y(0)
    vertical_scores((3, 4))
    values(3)
    swapped[2].wait_recv()
    project(2)
    relay_y(1)
    swapped[3].wait_recv()
    project(3)
    relay_y(2)
    project_own(0)
    relay_y(3)
    for unit in range(1, UNITS):
        project_own(unit)
    for unit in range(UNITS):
        total_up(unit)
    sends.finish()


def local(queries, prefix_kv, fresh_kv, group_blocks, head_pick, band_start, band_width, o_weight):
    vmem = pl.BlockSpec(memory_space=pltpu.VMEM)
    smem = pl.BlockSpec(memory_space=pltpu.SMEM)
    hbm = pl.BlockSpec(memory_space=pl.ANY)
    return pl.pallas_call(
        kernel,
        out_shape=jax.ShapeDtypeStruct((TOK, TOK), BF16),
        in_specs=[smem] * 4 + [hbm] * 4,
        out_specs=vmem,
        scratch_shapes=[
            pltpu.VMEM((PREFIX_DEV + FRESH_DEV, BLK, HD), BF16),
            pltpu.VMEM((PREFIX_DEV + FRESH_DEV, BLK, HD), BF16),
            pltpu.VMEM((2, WINDOW, BLK, HD), BF16),
            pltpu.VMEM((TOK, HEADS * HD), BF16),
            pltpu.VMEM((TOK, QH * HD), BF16),
            pltpu.VMEM((Y_SIZE, TOK, TOK), BF16),
            pltpu.VMEM((2, NG * BLK, HD), BF16),
            pltpu.VMEM((2, 2, HALF, HD), BF16),
            pltpu.VMEM((2, 2, QUARTER, HD), BF16),
            pltpu.VMEM((2, Z_SIZE - 1, PIECE, HD), BF16),
            pltpu.VMEM((2, NG * BLK, HD), BF16),
            pltpu.VMEM((BIAS_TILES, BLK, BLK), F32),
            pltpu.SMEM((CHUNKS, HEADS, NG + WINDOW), jnp.int32),
            pltpu.VMEM((CHUNKS, ROWS, BLK), F32),
            pltpu.VMEM((CHUNKS, ROWS, BLK), F32),
            pltpu.VMEM((CHUNKS, ROWS, HD), F32),
            pltpu.VMEM((ROWS, NG * BLK), F32),
            pltpu.VMEM((CHUNKS, ROWS, NG * BLK), BF16),
            pltpu.VMEM((TOK, HEADS * HD), BF16),
            pltpu.VMEM((TOK, HEADS * HD), BF16),
            pltpu.VMEM((3, TOK, TOK), BF16),
            pltpu.VMEM((UNITS, 2, TOK // UNITS // 2, TOK), F32),
            pltpu.VMEM((UNITS, TOK // UNITS, TOK), F32),
            pltpu.VMEM((UNITS, 2, TOK // UNITS // 2, TOK), BF16),
            pltpu.VMEM((2, TOK, TOK), BF16),
            pltpu.SemaphoreType.DMA((LOADS,)),
            pltpu.SemaphoreType.DMA((COPIES,)),
            pltpu.SemaphoreType.DMA((COPIES,)),
            pltpu.SemaphoreType.REGULAR,
        ],
        compiler_params=pltpu.CompilerParams(
            vmem_limit_bytes=56 * 2**20, collective_id=0, has_side_effects=True
        ),
    )(
        group_blocks,
        head_pick.T,
        band_start.T,
        band_width.T,
        queries,
        prefix_kv.reshape(2, PREFIX_DEV, BLK, HD),
        fresh_kv.reshape(2, FRESH_DEV, BLK, HD),
        o_weight,
    )


def solution(mesh):
    return jax.shard_map(
        local,
        mesh=mesh,
        in_specs=(
            P("ctx", "tp"),
            P(None, "ctx", "tp"),
            P(None, "ctx", "tp"),
            P(),
            P(),
            P(),
            P(),
            P("tp", None),
        ),
        out_specs=P("ctx", "tp"),
        check_vma=False,
    )
```
